512 devices in a mesh: sta: 32 (over y, z_lo), tm: 16 (over z_hi, x, core).
Axes of the slice: x: 4, y: 4, z: 16 (z_hi: 2, z_lo: 8; z = z_hi * 8 + z_lo), core: 2. Of those that a mesh axis runs over, the one named last changes fastest.
Arguments:
- records: bfloat16 [8192, 28800], P('sta', 'tm'), may hold values from -6 to 6
- validity: int32 [8192, 48], P('sta', 'tm'), may hold values from 0 to 1, as said below
- partners: int32 [32, 2], replicated, may hold values from -1 to 31, as said below
Outputs:
- correlation: float32 [8192, 2, 65, 256], P(('sta', 'tm'))
The draws below stay inside these ranges and needn't reach their ends.
Inputs may be any that keep to these rules, and one draw needn't show every extreme that they name: `partners`: entry 0 of row b is a block other than b at most 2 blocks away; entry 1 is -1 (no second partner) or another such block different from entry 0. `validity`: some stations have no usable window.
All inputs are finite; a program needn't handle non-finite values.
Results may differ from the reference program's by a relative error of at most 0.0046.
Values may be sent and summed in bfloat16 or wider, within the bound.
No kernel may reach another device: no remote copies, remote signals or barrier semaphores. Data moves between devices by JAX's collectives and lax.ppermute only.
A program may use at most 64 MiB of HBM per device.

```python
import math
import jax
import jax.numpy as jnp
from jax import lax

STA_DEV = 256
WIN = 600
BINS = 64
LAG = 32
SLOTS = 2
REACH = 2
LAGS = 65
BLOCKS = 32
STATIONS = 8192
WINDOWS = 48
SAMPLES = 28800


def draw_partners(key, part):
    key = jax.random.fold_in(key, 7)
    key_scores = jax.random.fold_in(key, 1)
    key_counts = jax.random.fold_in(key, 2)
    offsets = jnp.concatenate([jnp.arange(-REACH, 0, dtype=jnp.int32), jnp.arange(1, REACH + 1, dtype=jnp.int32)])
    blocks = jnp.arange(BLOCKS, dtype=jnp.int32)
    candidate = blocks[:, None] + offsets[None, :]
    inside = (candidate >= 0) & (candidate < BLOCKS)
    width_off = 2 * REACH
    scores = jax.random.randint(key_scores, (BLOCKS, width_off), 0, 1000) * width_off + jnp.arange(width_off, dtype=jnp.int32)[None, :]
    scores = jnp.where(inside, scores, -1)
    ranking = jnp.argsort(-scores, axis=1, stable=True)
    first_pick = jnp.take_along_axis(candidate, ranking[:, 0:1], axis=1)[:, 0]
    second = jnp.take_along_axis(candidate, ranking[:, 1:2], axis=1)[:, 0]
    pair_count = jax.random.randint(key_counts, (BLOCKS,), 1, 3)
    pair_count = jnp.where(blocks == 1, 2, pair_count)
    forced = (blocks == 0) | (blocks == 2) | (blocks == BLOCKS - 2) | (blocks == BLOCKS - 1)
    pair_count = jnp.where(forced, 1, pair_count)
    first_pick = jnp.where(blocks == 0, REACH, first_pick)
    first_pick = jnp.where(blocks == 2, 1, first_pick)
    first_pick = jnp.where(blocks == BLOCKS - 2, BLOCKS - 1, first_pick)
    first_pick = jnp.where(blocks == BLOCKS - 1, BLOCKS - 1 - REACH, first_pick)
    second = jnp.where(pair_count == 2, second, -1)
    return jnp.stack([first_pick, second], axis=1).astype(jnp.int32)


def draw_validity(key, part):
    key = jax.random.fold_in(key, 11)
    key_level = jax.random.fold_in(key, 1)
    key_cells = jax.random.fold_in(key, 2)
    key_silent = jax.random.fold_in(key, 3)
    raw_level = jax.random.randint(key_level, (STATIONS,), 0, 16)
    level = jnp.where(raw_level == 0, 0, 1 + raw_level % 4)
    silent = jax.random.randint(key_silent, (), 0, STATIONS)
    station_idx = jnp.arange(STATIONS, dtype=jnp.int32)
    level = jnp.where(station_idx == silent, 0, level)
    cells = jax.random.randint(key_cells, (STATIONS, WINDOWS), 0, 4)
    return (cells < level[:, None]).astype(jnp.int32)


def block_scale(stream_key, shape, pieces, smallest, top_value):
    factor_of, own = 1.0, jax.random.fold_in(stream_key, 6)
    for dim, shards_of in pieces:
        heights = jnp.exp(jax.random.uniform(jax.random.fold_in(own, dim), (shards_of,), jnp.float32, smallest / len(pieces), top_value / len(pieces)))
        factor_of = factor_of * jnp.repeat(heights, shape[dim] // shards_of).reshape([-1 if axis == dim else 1 for axis in range(len(shape))])
    return factor_of


def centred(key, dims, deviation, reach, cuts=(), kind=jnp.bfloat16):
    drawn = jax.random.normal(key, dims, jnp.float32) * deviation
    if len(cuts) > 0:
        drawn = block_scale(key, dims, cuts, -0.22, 0.18) * drawn
    return jnp.clip(drawn, min=-reach, max=reach).astype(kind)


def setup_inputs(seed: int = 0) -> dict:
    key_of = jax.random.split(jax.random.key(seed), 4)
    records = centred(key_of[0], (STATIONS, SAMPLES), 1.0, 6.0, ((0, 32), (1, 16)))
    validity = draw_validity(jax.random.fold_in(key_of[3], 71), 0)
    partners = draw_partners(jax.random.fold_in(key_of[3], 71), 0)
    return dict(records=records, validity=validity, partners=partners)


def forward_table(win_len, bin_count):
    sample_idx = jnp.arange(win_len, dtype=jnp.int32)
    harmonic = jnp.arange(1, bin_count + 1, dtype=jnp.int32)
    residue = sample_idx[:, None] * harmonic[None, :] % win_len
    phase_turns = residue.astype(jnp.float32) * (2.0 * math.pi / win_len)
    taper = 0.5 - 0.5 * jnp.cos((sample_idx.astype(jnp.float32) + 0.5) * (2.0 * math.pi / win_len))
    norm_factor = 1.0 / math.sqrt(win_len)
    table = jnp.concatenate([taper[:, None] * jnp.cos(phase_turns), -taper[:, None] * jnp.sin(phase_turns)], axis=1)
    return (table * norm_factor).astype(jnp.bfloat16)

def inverse_table(win_len, bin_count, max_lag):
    lag_values = jnp.arange(2 * max_lag + 1, dtype=jnp.int32) - max_lag
    harmonic = jnp.arange(1, bin_count + 1, dtype=jnp.int32)
    residue = jnp.mod(lag_values[:, None] * harmonic[None, :], win_len)
    phase_turns = residue.astype(jnp.float32) * (2.0 * math.pi / win_len)
    return jnp.concatenate([jnp.cos(phase_turns), -jnp.sin(phase_turns)], axis=1)

def whiten(spectra, maskf):
    bin_count = spectra.shape[-1] // 2
    real_part = spectra[..., :bin_count]
    imag_part = spectra[..., bin_count:]
    power_bins = real_part * real_part + imag_part * imag_part
    bin_idx = jnp.arange(bin_count, dtype=jnp.int32)
    nearby = (jnp.abs(bin_idx[:, None] - bin_idx[None, :]) <= 2).astype(jnp.float32)
    average = nearby / lax.optimization_barrier(jnp.sum(nearby, axis=0, keepdims=True))
    smooth = jnp.einsum('wsf,fg->wsg', power_bins, average, precision=lax.Precision.HIGHEST)
    inv_scale = 1.0 / jnp.sqrt(smooth + 0.05)
    inv_scale = jnp.concatenate([inv_scale, inv_scale], axis=-1)
    return (spectra * inv_scale * maskf[..., None]).astype(jnp.bfloat16)

def reference(records, validity, partners):
    table = forward_table(WIN, BINS).astype(jnp.float32)
    inverse = inverse_table(WIN, BINS, LAG)
    frames = records.reshape(BLOCKS, STA_DEV, WINDOWS, WIN)
    masks = validity.reshape(BLOCKS, STA_DEV, WINDOWS)

    def spectra_of(inputs):
        frame_block, mask_block = inputs
        spectra = jnp.einsum('swt,tc->wsc', frame_block.astype(jnp.float32), table)
        maskf = mask_block.T.astype(jnp.float32)
        return (whiten(spectra, maskf), maskf)
    white_all, mask_all = lax.map(spectra_of, (frames, masks))

    def per_block(block_id):
        own_white = white_all[block_id].astype(jnp.float32)
        own_mask = mask_all[block_id]
        real_own = own_white[..., :BINS]
        imag_own = own_white[..., BINS:]
        outputs = []
        for slot_id in range(SLOTS):
            target = partners[block_id, slot_id]
            present = (target >= 0).astype(jnp.float32)
            safe_target = jnp.maximum(target, 0)
            part_white = white_all[safe_target].astype(jnp.float32) * present
            part_mask = mask_all[safe_target] * present
            real_part = part_white[..., :BINS]
            imag_part = part_white[..., BINS:]
            cross_real = jnp.einsum('wif,wjf->ifj', real_own, real_part) + jnp.einsum('wif,wjf->ifj', imag_own, imag_part)
            cross_imag = jnp.einsum('wif,wjf->ifj', imag_own, real_part) - jnp.einsum('wif,wjf->ifj', real_own, imag_part)
            cross = jnp.concatenate([cross_real, cross_imag], axis=1)
            tallies = jnp.einsum('wi,wj->ij', own_mask, part_mask)
            lagged = jnp.einsum('tf,ifj->itj', inverse, cross, precision=lax.Precision.HIGHEST)
            outputs.append(lagged / jnp.maximum(tallies, 1.0)[:, None, :])
        return jnp.stack(outputs, axis=1)
    result = lax.map(per_block, jnp.arange(BLOCKS, dtype=jnp.int32))
    return result.reshape(STATIONS, SLOTS, LAGS, STA_DEV)
```

```python
import functools
import math

import jax
import jax.numpy as jnp
import numpy as np
from jax import lax
from jax.experimental import pallas as pl
from jax.experimental.pallas import tpu as pltpu
from jax.sharding import PartitionSpec as P

WIN = 600
BINS = 64
LAG = 32
SLOTS = 2
STA = 256
BLOCKS = 32
TM = 16
HALF = 8
CHIPS = 4
COLS = 2 * BINS
LAGS = 2 * LAG + 1
LPAD = 72
TALLY_ROW = LAGS
MASK_ROWS = 16
ROW_BLOCK = 128 // HALF
CHIP_ROWS = 2 * ROW_BLOCK
CHUNKS = (2, 1)
AXES = ("sta", "tm")
MIB = 1 << 20


def forward_table():
    sample = np.arange(WIN)
    harmonic = np.arange(1, BINS + 1)
    residue = sample[:, None] * harmonic[None, :] % WIN
    phase = residue.astype(np.float32) * np.float32(2.0 * math.pi / WIN)
    taper = np.float32(0.5) - np.float32(0.5) * np.cos(
        (sample.astype(np.float32) + np.float32(0.5)) * np.float32(2.0 * math.pi / WIN)
    )
    table = np.concatenate([taper[:, None] * np.cos(phase), -taper[:, None] * np.sin(phase)], axis=1)
    return (table * np.float32(1.0 / math.sqrt(WIN))).astype(jnp.bfloat16)


def window_spans(win_dev):
    total = win_dev * WIN
    spans = []
    for w in range(win_dev):
        lo = w * WIN // 128 * 128
        hi = min(-(-(w + 1) * WIN // 128) * 128, total)
        spans.append((lo, hi))
    return spans


def window_tables(win_dev):
    table = forward_table()
    out = []
    for w, (lo, hi) in enumerate(window_spans(win_dev)):
        padded = np.zeros((hi - lo, COLS), table.dtype)
        padded[w * WIN - lo : (w + 1) * WIN - lo] = table
        out.append(np.ascontiguousarray(padded.T))
    return out


def band_average():
    bins = np.arange(BINS)
    nearby = (np.abs(bins[:, None] - bins[None, :]) <= 2).astype(np.float32)
    return np.ascontiguousarray((nearby / nearby.sum(axis=0, keepdims=True)).T)


def lag_tables():
    lags = np.arange(LAGS) - LAG
    harmonic = np.arange(1, BINS + 1)
    phase = np.mod(lags[:, None] * harmonic[None, :], WIN) * (2.0 * math.pi / WIN)
    cosine = np.zeros((LPAD, COLS), np.float32)
    sine = np.zeros((LPAD, COLS), np.float32)
    cosine[:LAGS] = np.tile(np.cos(phase), (1, 2))
    sine[:LAGS] = np.concatenate([-np.sin(phase), np.sin(phase)], axis=1)
    return cosine, sine


def routes(target):
    pairs = []
    for b in range(BLOCKS):
        for t in range(TM):
            there = target(b, t)
            if there is not None:
                pairs.append((b * TM + t, there[0] * TM + there[1]))
    return pairs


def to_other_half(b, t):
    return b, (t + HALF) % TM


def to_block(by):
    def target(b, t):
        nb = b + by
        if not 0 <= nb < BLOCKS:
            return None
        return nb, t if nb // 8 == b // 8 else (t + HALF) % TM

    return target


def to_chip(by):
    return lambda b, t: (b, t // HALF * HALF + (t % HALF // 2 + by) % CHIPS * 2 + t % 2)


def to_core(b, t):
    return b, t ^ 1


def send(array, target):
    return lax.ppermute(array, AXES, routes(target))


CHIP_GROUPS = [[z * HALF + 2 * i + c for i in range(CHIPS)] for z in range(TM // HALF) for c in range(2)]


def whiten_kernel(spans, rec_ref, mask_ref, avg_ref, *refs):
    win_dev = len(spans)
    tables, outs = refs[:win_dev], refs[win_dev:]
    mask = mask_ref[...]
    w = 0
    for part, windows in enumerate(CHUNKS):
        for k in range(windows):
            lo, hi = spans[w]
            spectra = lax.dot_general(
                tables[w][...], rec_ref[:, lo:hi], (((1,), (1,)), ((), ())), preferred_element_type=jnp.float32
            )
            real, imag = spectra[:BINS], spectra[BINS:]
            power = real * real + imag * imag
            smooth = jnp.dot(avg_ref[...], power, precision=lax.Precision.HIGHEST, preferred_element_type=jnp.float32)
            scale = mask[w : w + 1] / jnp.sqrt(smooth + 0.05)
            outs[part][k * COLS : k * COLS + BINS] = (real * scale).astype(jnp.bfloat16)
            outs[part][k * COLS + BINS : (k + 1) * COLS] = (imag * scale).astype(jnp.bfloat16)
            w += 1
    outs[0][CHUNKS[0] * COLS :] = mask.astype(jnp.bfloat16)


def whitened(records, validity):
    rows, samples = records.shape
    win_dev = validity.shape[1]
    spans = window_spans(win_dev)
    mask = jnp.pad(validity.T.astype(jnp.float32), ((0, MASK_ROWS - win_dev), (0, 0)))
    vmem = pl.BlockSpec(memory_space=pltpu.VMEM)
    shapes = [
        jax.ShapeDtypeStruct((n * COLS + (MASK_ROWS if i == 0 else 0), rows), jnp.bfloat16)
        for i, n in enumerate(CHUNKS)
    ]
    return pl.pallas_call(
        functools.partial(whiten_kernel, spans),
        out_shape=shapes,
        in_specs=[vmem] * (3 + win_dev),
        out_specs=[vmem] * len(shapes),
        compiler_params=pltpu.CompilerParams(vmem_limit_bytes=16 * MIB),
        name="whiten",
    )(records, mask, band_average(), *window_tables(win_dev))


def rotate_kernel(groups, own_ref, cos_ref, sin_ref, out_ref):
    cosine, sine = cos_ref[...], sin_ref[...]
    for m in range(own_ref.shape[0]):
        for g in range(groups):
            lanes = slice(g * COLS, (g + 1) * COLS)
            row = own_ref[m : m + 1, lanes]
            other = pltpu.roll(row, BINS, 1)
            out_ref[m * LPAD : (m + 1) * LPAD, lanes] = (row * cosine + other * sine).astype(jnp.bfloat16)


def rotated(own):
    stations, width = own.shape
    cosine, sine = lag_tables()
    step = 8
    return pl.pallas_call(
        functools.partial(rotate_kernel, width // COLS),
        out_shape=jax.ShapeDtypeStruct((stations * LPAD, width), jnp.bfloat16),
        grid=(stations // step,),
        in_specs=[
            pl.BlockSpec((step, width), lambda i: (i, 0)),
            pl.BlockSpec((LPAD, COLS), lambda i: (0, 0)),
            pl.BlockSpec((LPAD, COLS), lambda i: (0, 0)),
        ],
        out_specs=pl.BlockSpec((step * LPAD, width), lambda i: (i, 0)),
        compiler_params=pltpu.CompilerParams(vmem_limit_bytes=32 * MIB),
        cost_estimate=pl.CostEstimate(
            flops=3 * stations * LPAD * width, bytes_accessed=2 * stations * LPAD * width, transcendentals=0
        ),
        name="rotate",
    )(own, cosine, sine)


def lags_kernel(depth, pieces, has_acc, has_tally, turned_ref, *refs):
    far = refs[:pieces]
    refs = refs[pieces:]
    out_ref = refs[-1]
    total = refs[0][...].astype(jnp.float32) if has_acc else None
    for d in range(pieces):
        term = jnp.dot(
            turned_ref[:, d * depth : (d + 1) * depth], far[d][:depth], preferred_element_type=jnp.float32
        )
        total = term if total is None else total + term
    out_ref[...] = total.astype(out_ref.dtype)
    if has_tally:
        tally_ref = refs[1 if has_acc else 0]
        for m in range(tally_ref.shape[0]):
            row = m * LPAD + TALLY_ROW
            out_ref[row : row + 1] = tally_ref[m : m + 1].astype(out_ref.dtype)


def into_lags(turned, far, depth, first, count, acc=None, tally=None, dtype=jnp.float32):
    width = far[0].shape[1]
    step = 8
    base = first // step
    rows = step * LPAD
    args = [turned, *far]
    specs = [pl.BlockSpec((rows, turned.shape[1]), lambda i: (base + i, 0))]
    specs += [pl.BlockSpec(f.shape, lambda i: (0, 0)) for f in far]
    if acc is not None:
        args.append(acc)
        specs.append(pl.BlockSpec((rows, width), lambda i: (base + i, 0)))
    if tally is not None:
        args.append(tally)
        specs.append(pl.BlockSpec((step, width), lambda i: (base + i, 0)))
    return pl.pallas_call(
        functools.partial(lags_kernel, depth, len(far), acc is not None, tally is not None),
        out_shape=jax.ShapeDtypeStruct((count * LPAD, width), dtype),
        grid=(count // step,),
        in_specs=specs,
        out_specs=pl.BlockSpec((rows, width), lambda i: (i, 0)),
        compiler_params=pltpu.CompilerParams(vmem_limit_bytes=40 * MIB),
        cost_estimate=pl.CostEstimate(
            flops=2 * count * LPAD * width * depth * len(far),
            bytes_accessed=2 * count * LPAD * turned.shape[1] + 4 * count * LPAD * width,
            transcendentals=0,
        ),
        name="lags",
    )(*args)


def combine_kernel(mine_ref, theirs_ref, out_ref):
    for m in range(out_ref.shape[0]):
        rows = slice(m * LPAD, (m + 1) * LPAD)
        total = mine_ref[rows] + theirs_ref[rows].astype(jnp.float32)
        result = total[:LAGS] / jnp.maximum(total[TALLY_ROW : TALLY_ROW + 1], 1.0)
        for q in range(SLOTS):
            out_ref[m, q] = result[:, q * STA : (q + 1) * STA]


def combined(mine, theirs):
    stations = mine.shape[0] // LPAD
    step = 4
    block = pl.BlockSpec((step * LPAD, mine.shape[1]), lambda i: (i, 0))
    return pl.pallas_call(
        combine_kernel,
        out_shape=jax.ShapeDtypeStruct((stations, SLOTS, LAGS, STA), jnp.float32),
        grid=(stations // step,),
        in_specs=[block, block],
        out_specs=pl.BlockSpec((step, SLOTS, LAGS, STA), lambda i: (i, 0, 0, 0)),
        compiler_params=pltpu.CompilerParams(vmem_limit_bytes=16 * MIB),
        name="combine",
    )(mine, theirs)


def body(records, validity, partners):
    place = lax.axis_index("tm")
    z_hi, chip, core = place // HALF, place % HALF // 2, place % 2
    block_id = lax.axis_index("sta")
    pair = lax.dynamic_index_in_dim(partners, block_id, 0, keepdims=False)

    parts = []
    for i, white in enumerate(whitened(records, validity)):
        other = send(white, to_other_half)
        first = jnp.where(z_hi == 0, white, other)
        second = jnp.where(z_hi == 0, other, white)
        depth = CHUNKS[i] * COLS
        parts.append(jnp.concatenate([first[:depth], second[:depth], first[depth:], second[depth:]], axis=0))

    mine = [lax.dynamic_slice_in_dim(part, z_hi * 128, 128, axis=1) for part in parts]
    rows = jnp.concatenate(mine, axis=0).T.reshape(CHIPS, CHIP_ROWS, -1)
    rows = lax.all_to_all(rows, "tm", 0, 0, axis_index_groups=CHIP_GROUPS, tiled=True)
    order = (chip + jnp.array([0, CHIPS - 1, 1, 2])) % CHIPS
    rows = jnp.take(rows, order, axis=0, mode="clip")
    rows = jnp.where(core == 0, jnp.roll(rows, ROW_BLOCK, axis=1), rows)
    rows = rows.transpose(1, 0, 2)

    turned, own_mask, at = [], None, 0
    for i, windows in enumerate(CHUNKS):
        depth = 2 * windows * COLS
        own = rows[:, :, at : at + depth].reshape(CHIP_ROWS, CHIPS * depth)
        turned.append(rotated(own.astype(jnp.float32)))
        at += depth
        if i == 0:
            own_mask = rows[:, :, at : at + 2 * MASK_ROWS].reshape(CHIP_ROWS, -1)
            at += 2 * MASK_ROWS

    far = []
    for part in parts:
        near = {-1: send(part, to_block(1)), 1: send(part, to_block(-1))}
        near[-2] = send(near[-1], to_block(1))
        near[2] = send(near[1], to_block(-1))
        chosen = []
        for q in range(SLOTS):
            picked = jnp.zeros_like(part)
            for by, array in near.items():
                picked = jnp.where((pair[q] == block_id + by) & (pair[q] >= 0), array, picked)
            chosen.append(picked)
        held = jnp.concatenate(chosen, axis=1)
        far.append([held, send(held, to_chip(1)), send(held, to_chip(-1)), send(held, to_chip(2))])

    depth = 2 * CHUNKS[0] * COLS
    far_mask = jnp.concatenate([piece[depth:] for piece in far[0]], axis=0)
    tally = jnp.dot(own_mask, far_mask, preferred_element_type=jnp.float32)

    acc = None
    for i in range(len(CHUNKS) - 1):
        acc = into_lags(turned[i], far[i], 2 * CHUNKS[i] * COLS, 0, CHIP_ROWS, acc)
    last = functools.partial(into_lags, turned[-1], far[-1], 2 * CHUNKS[-1] * COLS, acc=acc, tally=tally)
    theirs = send(last(0, ROW_BLOCK, dtype=jnp.bfloat16), to_core)
    return combined(last(ROW_BLOCK, ROW_BLOCK), theirs)


def solution(mesh):
    return jax.shard_map(
        body,
        mesh=mesh,
        in_specs=(P("sta", "tm"), P("sta", "tm"), P()),
        out_specs=P(("sta", "tm"), None, None, None),
        check_vma=False,
    )
```

```python
import functools
import math

import jax
import jax.numpy as jnp
import numpy as np
from jax import lax
from jax.experimental import pallas as pl
from jax.experimental.pallas import tpu as pltpu
from jax.sharding import PartitionSpec as P

WIN = 600
BINS = 64
LAG = 32
SLOTS = 2
STA = 256
BLOCKS = 32
TM = 16
HALF = 8
CHIPS = 4
COLS = 2 * BINS
LAGS = 2 * LAG + 1
LPAD = 72
TALLY_ROW = LAGS
MASK_ROWS = 16
ROW_BLOCK = 128 // HALF
CHIP_ROWS = 2 * ROW_BLOCK
WHITE = 3 * COLS
SENT = WHITE + MASK_ROWS
WIDE = WHITE + 128
TURNS = (0, 1, -1, 2)
TILE = 8 * LPAD
DEEP = CHIPS * WHITE
SPAN = 616
AXES = ("sta", "tm")
MIB = 1 << 20


def forward_table():
    sample = np.arange(WIN)
    harmonic = np.arange(1, BINS + 1)
    residue = sample[:, None] * harmonic[None, :] % WIN
    phase = residue.astype(np.float32) * np.float32(2.0 * math.pi / WIN)
    taper = np.float32(0.5) - np.float32(0.5) * np.cos(
        (sample.astype(np.float32) + np.float32(0.5)) * np.float32(2.0 * math.pi / WIN)
    )
    table = np.concatenate([taper[:, None] * np.cos(phase), -taper[:, None] * np.sin(phase)], axis=1)
    return (table * np.float32(1.0 / math.sqrt(WIN))).astype(jnp.bfloat16)


def window_start(w):
    return w * (WIN // 16 * 16)


def window_tables(win_dev):
    table = forward_table()
    out = np.zeros((win_dev, COLS, SPAN), table.dtype)
    for w in range(win_dev):
        at = w * WIN - window_start(w)
        out[w, :, at : at + WIN] = table.T
    return out


def band_average():
    bins = np.arange(BINS)
    nearby = (np.abs(bins[:, None] - bins[None, :]) <= 2).astype(np.float32)
    return np.ascontiguousarray((nearby / nearby.sum(axis=0, keepdims=True)).T)


def lag_tables():
    lags = np.arange(LAGS) - LAG
    harmonic = np.arange(1, BINS + 1)
    phase = np.mod(lags[:, None] * harmonic[None, :], WIN) * (2.0 * math.pi / WIN)
    cosine = np.zeros((LPAD, COLS), np.float32)
    sine = np.zeros((LPAD, COLS), np.float32)
    cosine[:LAGS] = np.tile(np.cos(phase), (1, 2))
    sine[:LAGS] = np.concatenate([-np.sin(phase), np.sin(phase)], axis=1)
    return cosine, sine


def routes(target):
    pairs = []
    for b in range(BLOCKS):
        for t in range(TM):
            there = target(b, t)
            if there is not None:
                pairs.append((b * TM + t, there[0] * TM + there[1]))
    return pairs


def to_other_half(b, t):
    return b, (t + HALF) % TM


def to_block(by):
    def target(b, t):
        nb = b + by
        if not 0 <= nb < BLOCKS:
            return None
        return nb, t if nb // 8 == b // 8 else (t + HALF) % TM

    return target


def to_chip(by):
    return lambda b, t: (b, t // HALF * HALF + (t % HALF // 2 + by) % CHIPS * 2 + t % 2)


def to_core(b, t):
    return b, t ^ 1


def send(array, target):
    return lax.ppermute(array, AXES, routes(target))


VMEM = pl.BlockSpec(memory_space=pltpu.VMEM)
SMEM = pl.BlockSpec(memory_space=pltpu.SMEM)
ANY = pl.BlockSpec(memory_space=pl.ANY)


def store_rows(out_ref, white, z_hi):
    lanes = pl.ds(pl.multiple_of(z_hi * 128, 128), 128)
    for g in range(WHITE // COLS):
        block = white[g * COLS : (g + 1) * COLS, lanes].astype(jnp.float32)
        out_ref[:, g * COLS : (g + 1) * COLS] = block.T.astype(jnp.bfloat16)
    mask = white[WHITE:SENT, lanes].astype(jnp.float32)
    mask = jnp.concatenate([mask, jnp.zeros((128 - MASK_ROWS, 128), jnp.float32)], axis=0)
    out_ref[:, WHITE:] = mask.T.astype(jnp.bfloat16)


def whiten_kernel(place_ref, rec_hbm, mask_hbm, avg_hbm, table_hbm, out_ref, rows_ref, rec, mask_in, avg, table, sems):
    win_dev = table_hbm.shape[0]
    copies = [pltpu.make_async_copy(mask_hbm, mask_in, sems.at[0]), pltpu.make_async_copy(avg_hbm, avg, sems.at[1])]
    for w in range(win_dev):
        copies.append(pltpu.make_async_copy(table_hbm.at[w], table.at[w], sems.at[2 + 2 * w]))
        samples = pl.ds(window_start(w), SPAN)
        copies.append(pltpu.make_async_copy(rec_hbm.at[samples], rec.at[w], sems.at[3 + 2 * w]))
    for copy in copies:
        copy.start()
    copies[0].wait()
    copies[1].wait()
    mask = mask_in[...].astype(jnp.float32)
    for w in range(win_dev):
        copies[2 + 2 * w].wait()
        copies[3 + 2 * w].wait()
        spectra = jnp.dot(table[w], rec[w], preferred_element_type=jnp.float32)
        real, imag = spectra[:BINS], spectra[BINS:]
        power = real * real + imag * imag
        smooth = jnp.dot(avg[...], power, precision=lax.Precision.HIGHEST, preferred_element_type=jnp.float32)
        scale = mask[w : w + 1] / jnp.sqrt(smooth + 0.05)
        out_ref[w * COLS : w * COLS + BINS] = (real * scale).astype(jnp.bfloat16)
        out_ref[w * COLS + BINS : (w + 1) * COLS] = (imag * scale).astype(jnp.bfloat16)
    empty = jnp.zeros((MASK_ROWS - win_dev, STA), jnp.float32)
    out_ref[WHITE:] = jnp.concatenate([mask, empty], axis=0).astype(jnp.bfloat16)
    store_rows(rows_ref, out_ref, place_ref[0])


def whitened(place, records, validity):
    rows, win_dev = validity.shape
    return pl.pallas_call(
        whiten_kernel,
        out_shape=[
            jax.ShapeDtypeStruct((SENT, rows), jnp.bfloat16),
            jax.ShapeDtypeStruct((128, WIDE), jnp.bfloat16),
        ],
        in_specs=[SMEM, ANY, ANY, ANY, ANY],
        out_specs=[VMEM, VMEM],
        scratch_shapes=[
            pltpu.VMEM((win_dev, SPAN, rows), records.dtype),
            pltpu.VMEM((win_dev, rows), jnp.int32),
            pltpu.VMEM((BINS, BINS), jnp.float32),
            pltpu.VMEM((win_dev, COLS, SPAN), jnp.bfloat16),
            pltpu.SemaphoreType.DMA((2 + 2 * win_dev,)),
        ],
        compiler_params=pltpu.CompilerParams(vmem_limit_bytes=60 * MIB),
        name="whiten",
    )(place, records.T, validity.T, band_average(), window_tables(win_dev))


def choose_kernel(choice_ref, place_ref, *refs):
    blocks, refs = refs[:4], refs[4:]
    outs = refs
    if len(refs) > 1:
        rows_ref, other_ref, other_rows = refs[0], refs[1], refs[-1]
        outs = refs[2:-1]
        store_rows(other_rows, other_ref, place_ref[0])
    for q in range(SLOTS):
        rows = slice(q * SENT, (q + 1) * SENT)

        @pl.when(choice_ref[q] == 0)
        def _():
            for out_ref in outs:
                out_ref[rows] = jnp.zeros((SENT, STA), jnp.bfloat16)

        for k, ref in enumerate(blocks):

            @pl.when(choice_ref[q] == k + 1)
            def _():
                for out_ref in outs:
                    out_ref[rows] = ref[...]

    if len(refs) > 1:
        for by, out_ref in zip(TURNS, outs):
            chip = lax.rem(place_ref[1] + CHIPS + by, CHIPS)
            stations = pl.ds(pl.multiple_of(chip * CHIP_ROWS, CHIP_ROWS), CHIP_ROWS)
            at = SLOTS * SENT
            for source in (rows_ref, other_rows):
                for lanes in (slice(0, STA), slice(STA, WIDE)):
                    out_ref[at : at + CHIP_ROWS] = source[stations, lanes]
                    at += CHIP_ROWS


def chosen(choice, place, blocks, own=()):
    rows = SLOTS * SENT + (4 * CHIP_ROWS if own else 0)
    count = CHIPS if own else 1
    return pl.pallas_call(
        choose_kernel,
        out_shape=[jax.ShapeDtypeStruct((rows, STA), jnp.bfloat16)] * count,
        in_specs=[SMEM, SMEM] + [VMEM] * (len(blocks) + len(own)),
        out_specs=[VMEM] * count,
        scratch_shapes=[pltpu.VMEM((128, WIDE), jnp.bfloat16)] if own else [],
        compiler_params=pltpu.CompilerParams(vmem_limit_bytes=6 * MIB),
        name="choose",
    )(choice, place, *blocks, *own)


def turn_kernel(place_ref, *refs):
    far, (cos_ref, sin_ref, out_ref, mask_ref, held) = refs[:CHIPS], refs[CHIPS:]
    core = place_ref[2]
    cosine, sine = cos_ref[...], sin_ref[...]
    for half in range(2):
        at = SLOTS * SENT + half * 2 * CHIP_ROWS
        for d in range(CHIPS):
            for h, whose in enumerate((1 - core, core)):
                here = slice(h * ROW_BLOCK, (h + 1) * ROW_BLOCK)
                for part in range(2):
                    start = pl.multiple_of(at + part * CHIP_ROWS + whose * ROW_BLOCK, ROW_BLOCK)
                    rows = far[d][pl.ds(start, ROW_BLOCK)]
                    held[d, here, part * STA : (part + 1) * STA] = rows.astype(jnp.float32)
        mask = held[0, :, WHITE:]
        for d in range(1, CHIPS):
            mask += pltpu.roll(held[d, :, WHITE:], d * MASK_ROWS, 1)
        mask_ref[half] = mask.astype(jnp.bfloat16)

        def eight(i, carry):
            stations = pl.ds(pl.multiple_of(i * 8, 8), 8)
            for d in range(CHIPS):
                for g in range(WHITE // COLS):
                    block = held[d, stations, g * COLS : (g + 1) * COLS]
                    swapped = pltpu.roll(block, BINS, 1)
                    lanes = slice(d * WHITE + g * COLS, d * WHITE + (g + 1) * COLS)
                    for k in range(0, 8, 2):
                        turned = [block[m : m + 1] * cosine + swapped[m : m + 1] * sine for m in (k, k + 1)]
                        at = pl.multiple_of(i * TILE + k * LPAD, 2 * LPAD)
                        out_ref[half, pl.ds(at, 2 * LPAD), lanes] = jnp.concatenate(turned, axis=0).astype(jnp.bfloat16)
            return carry

        lax.fori_loop(0, CHIP_ROWS // 8, eight, 0)


def turned_rows(place, far):
    cosine, sine = lag_tables()
    height = CHIP_ROWS * LPAD
    return pl.pallas_call(
        turn_kernel,
        out_shape=[
            jax.ShapeDtypeStruct((2, height, DEEP), jnp.bfloat16),
            jax.ShapeDtypeStruct((2, CHIP_ROWS, 128), jnp.bfloat16),
        ],
        in_specs=[SMEM] + [VMEM] * (CHIPS + 2),
        out_specs=[VMEM, VMEM],
        scratch_shapes=[pltpu.VMEM((CHIPS, CHIP_ROWS, WIDE), jnp.float32)],
        compiler_params=pltpu.CompilerParams(vmem_limit_bytes=18 * MIB),
        cost_estimate=pl.CostEstimate(flops=6 * height * DEEP, bytes_accessed=4 * height * DEEP, transcendentals=0),
        name="turn",
    )(place, *far, cosine, sine)


def lags_kernel(half, first, count, has_acc, choice_ref, turned_ref, valid_ref, *refs):
    far = refs[:CHIPS]
    acc_ref = refs[CHIPS] if has_acc else None
    out_ref = refs[-1]
    which = [(choice_ref[SLOTS + q] + half) % 2 for q in range(SLOTS)]

    def tile(i, carry):
        source = pl.ds(pl.multiple_of(first * LPAD + i * TILE, TILE), TILE)
        target = pl.ds(pl.multiple_of(i * TILE, TILE), TILE)
        for q in range(SLOTS):
            lanes = slice(q * STA, (q + 1) * STA)
            piece = jnp.concatenate([ref[q * SENT : q * SENT + WHITE] for ref in far], axis=0)
            total = jnp.dot(turned_ref[which[q], source], piece, preferred_element_type=jnp.float32)
            if has_acc:
                total += acc_ref[source, lanes]
            out_ref[target, lanes] = total.astype(out_ref.dtype)
        return carry

    lax.fori_loop(0, count * LPAD // TILE, tile, 0)
    for q in range(SLOTS):
        lanes = slice(q * STA, (q + 1) * STA)
        mask = jnp.concatenate([ref[q * SENT + WHITE : (q + 1) * SENT] for ref in far], axis=0)
        valid = valid_ref[which[q], first : first + count, : CHIPS * MASK_ROWS]
        tally = jnp.dot(valid, mask, preferred_element_type=jnp.float32)
        for m in range(count):
            row = m * LPAD + TALLY_ROW
            value = tally[m : m + 1]
            if has_acc:
                value += acc_ref[first * LPAD + row : first * LPAD + row + 1, lanes]
            out_ref[row : row + 1, lanes] = value.astype(out_ref.dtype)


def into_lags(choice, own, far, half, first, count, acc=None, dtype=jnp.float32):
    args = [choice, *own, *far] + ([] if acc is None else [acc])
    return pl.pallas_call(
        functools.partial(lags_kernel, half, first, count, acc is not None),
        out_shape=jax.ShapeDtypeStruct((count * LPAD, SLOTS * STA), dtype),
        in_specs=[SMEM] + [VMEM] * (len(args) - 1),
        out_specs=VMEM,
        compiler_params=pltpu.CompilerParams(vmem_limit_bytes=8 * MIB),
        cost_estimate=pl.CostEstimate(
            flops=2 * count * LPAD * SLOTS * STA * DEEP,
            bytes_accessed=4 * count * LPAD * SLOTS * STA,
            transcendentals=0,
        ),
        name="lags",
    )(*args)


def combine_kernel(mine_ref, theirs_ref, out_ref):
    for m in range(out_ref.shape[0]):
        rows = slice(m * LPAD, (m + 1) * LPAD)
        total = mine_ref[rows] + theirs_ref[rows].astype(jnp.float32)
        result = total[:LAGS] / jnp.maximum(total[TALLY_ROW : TALLY_ROW + 1], 1.0)
        for q in range(SLOTS):
            out_ref[m, :, q] = result[:, q * STA : (q + 1) * STA]


def combined(mine, theirs):
    stations = mine.shape[0] // LPAD
    step = 4
    block = pl.BlockSpec((step * LPAD, mine.shape[1]), lambda i: (i, 0))
    out = pl.pallas_call(
        combine_kernel,
        out_shape=jax.ShapeDtypeStruct((stations, LAGS, SLOTS, STA), jnp.float32),
        grid=(stations // step,),
        in_specs=[block, block],
        out_specs=pl.BlockSpec((step, LAGS, SLOTS, STA), lambda i: (i, 0, 0, 0)),
        compiler_params=pltpu.CompilerParams(vmem_limit_bytes=8 * MIB),
        name="combine",
    )(mine, theirs)
    return out.transpose(0, 2, 1, 3)


def body(records, validity, partners):
    index = lax.axis_index("tm")
    place = jnp.stack([index // HALF, index % HALF // 2, index % 2])
    block_id = lax.axis_index("sta")
    pair = lax.dynamic_index_in_dim(partners, block_id, 0, keepdims=False)
    by = pair - block_id
    choice = jnp.where(by == -1, 1, jnp.where(by == 1, 2, jnp.where(by == -2, 3, jnp.where(by == 2, 4, 0))))
    choice = jnp.where(pair >= 0, choice, 0)
    choice = jnp.concatenate([choice, (pair // 8 != block_id // 8).astype(jnp.int32)])

    def neighbours(white):
        back, on = send(white, to_block(1)), send(white, to_block(-1))
        return [back, on, send(back, to_block(1)), send(on, to_block(-1))]

    def to_chips(arrays):
        return [arrays[0]] + [send(array, to_chip(by)) for by, array in zip(TURNS[1:], arrays[1:])]

    white, rows = whitened(place, records, validity)
    other = send(white, to_other_half)
    far = to_chips(chosen(choice, place, neighbours(white), (rows, other)))
    other_far = to_chips(chosen(choice, place, neighbours(other)) * CHIPS)
    own = turned_rows(place, far)

    acc = into_lags(choice, own, far, 0, 0, CHIP_ROWS)
    last = functools.partial(into_lags, choice, own, other_far, 1, acc=acc)
    theirs = send(last(0, ROW_BLOCK, dtype=jnp.bfloat16), to_core)
    return combined(last(ROW_BLOCK, ROW_BLOCK), theirs)


def solution(mesh):
    return jax.shard_map(
        body,
        mesh=mesh,
        in_specs=(P("sta", "tm"), P("sta", "tm"), P()),
        out_specs=P(("sta", "tm"), None, None, None),
        check_vma=False,
    )
```

```python
import functools
import math

import jax
import jax.numpy as jnp
import numpy as np
from jax import lax
from jax.experimental import pallas as pl
from jax.experimental.pallas import tpu as pltpu
from jax.sharding import PartitionSpec as P

WIN = 600
BINS = 64
LAG = 32
SLOTS = 2
STA = 256
BLOCKS = 32
TM = 16
HALF = 8
CHIPS = 4
COLS = 2 * BINS
LAGS = 2 * LAG + 1
LPAD = 72
TALLY_ROW = LAGS
MASK_ROWS = 16
ROW_BLOCK = 128 // HALF
CHIP_ROWS = 2 * ROW_BLOCK
WHITE = 3 * COLS
SENT = WHITE + MASK_ROWS
WIDE = WHITE + 128
OWN = 4 * CHIP_ROWS
TURNS = (0, 1, -1, 2)
TILE = 8 * LPAD
DEEP = CHIPS * WHITE
SPAN = 616
AXES = ("sta", "tm")
MIB = 1 << 20


def forward_table():
    sample = np.arange(WIN)
    harmonic = np.arange(1, BINS + 1)
    residue = sample[:, None] * harmonic[None, :] % WIN
    phase = residue.astype(np.float32) * np.float32(2.0 * math.pi / WIN)
    taper = np.float32(0.5) - np.float32(0.5) * np.cos(
        (sample.astype(np.float32) + np.float32(0.5)) * np.float32(2.0 * math.pi / WIN)
    )
    table = np.concatenate([taper[:, None] * np.cos(phase), -taper[:, None] * np.sin(phase)], axis=1)
    return (table * np.float32(1.0 / math.sqrt(WIN))).astype(jnp.bfloat16)


def window_start(w):
    return w * (WIN // 16 * 16)


def window_tables(win_dev):
    table = forward_table()
    out = np.zeros((win_dev, COLS, SPAN), table.dtype)
    for w in range(win_dev):
        at = w * WIN - window_start(w)
        out[w, :, at : at + WIN] = table.T
    return out


def band_average():
    bins = np.arange(BINS)
    nearby = (np.abs(bins[:, None] - bins[None, :]) <= 2).astype(np.float32)
    return np.ascontiguousarray((nearby / nearby.sum(axis=0, keepdims=True)).T)


def lag_tables():
    lags = np.arange(LAGS) - LAG
    harmonic = np.arange(1, BINS + 1)
    phase = np.mod(lags[:, None] * harmonic[None, :], WIN) * (2.0 * math.pi / WIN)
    cosine = np.zeros((LPAD, COLS), np.float32)
    sine = np.zeros((LPAD, COLS), np.float32)
    cosine[:LAGS] = np.tile(np.cos(phase), (1, 2))
    sine[:LAGS] = np.concatenate([-np.sin(phase), np.sin(phase)], axis=1)
    return np.stack([cosine, sine])


def routes(target):
    pairs = []
    for b in range(BLOCKS):
        for t in range(TM):
            there = target(b, t)
            if there is not None:
                pairs.append((b * TM + t, there[0] * TM + there[1]))
    return pairs


def to_other_half(b, t):
    return b, (t + HALF) % TM


def to_block(by):
    def target(b, t):
        nb = b + by
        if not 0 <= nb < BLOCKS:
            return None
        return nb, t if nb // 8 == b // 8 else (t + HALF) % TM

    return target


def to_chip(by):
    return lambda b, t: (b, t // HALF * HALF + (t % HALF // 2 + by) % CHIPS * 2 + t % 2)


def to_core(b, t):
    return b, t ^ 1


def send(array, target):
    return lax.ppermute(array, AXES, routes(target))


CHIP_GROUPS = [[z * HALF + 2 * i + c for i in range(CHIPS)] for z in range(TM // HALF) for c in range(2)]


VMEM = pl.BlockSpec(memory_space=pltpu.VMEM)
SMEM = pl.BlockSpec(memory_space=pltpu.SMEM)
ANY = pl.BlockSpec(memory_space=pl.ANY)


def place():
    index = lax.axis_index("tm")
    return index // HALF, index % HALF // 2, index % 2


def partner(partners_ref, q):
    block = lax.axis_index("sta")
    target = partners_ref[q, block]
    return block, target, jnp.where(target // 8 == block // 8, 0, 1)


def whiten_kernel(rec_hbm, mask_hbm, avg_hbm, table_hbm, out_ref, rec, mask_in, avg, table, sems):
    win_dev = table_hbm.shape[0]
    copies = [pltpu.make_async_copy(mask_hbm, mask_in, sems.at[0]), pltpu.make_async_copy(avg_hbm, avg, sems.at[1])]
    for w in range(win_dev):
        copies.append(pltpu.make_async_copy(table_hbm.at[w], table.at[w], sems.at[2 + 2 * w]))
        samples = pl.ds(window_start(w), SPAN)
        copies.append(pltpu.make_async_copy(rec_hbm.at[samples], rec.at[w], sems.at[3 + 2 * w]))
    for copy in copies:
        copy.start()
    copies[0].wait()
    copies[1].wait()
    mask = mask_in[...].astype(jnp.float32)
    for w in range(win_dev):
        copies[2 + 2 * w].wait()
        copies[3 + 2 * w].wait()
        spectra = jnp.dot(table[w], rec[w], preferred_element_type=jnp.float32)
        real, imag = spectra[:BINS], spectra[BINS:]
        power = real * real + imag * imag
        smooth = jnp.dot(avg[...], power, precision=lax.Precision.HIGHEST, preferred_element_type=jnp.float32)
        scale = mask[w : w + 1] / jnp.sqrt(smooth + 0.05)
        out_ref[w * COLS : w * COLS + BINS] = (real * scale).astype(jnp.bfloat16)
        out_ref[w * COLS + BINS : (w + 1) * COLS] = (imag * scale).astype(jnp.bfloat16)
    empty = jnp.zeros((MASK_ROWS - win_dev, STA), jnp.float32)
    out_ref[WHITE:] = jnp.concatenate([mask, empty], axis=0).astype(jnp.bfloat16)


def whitened(records, validity):
    rows, win_dev = validity.shape
    return pl.pallas_call(
        whiten_kernel,
        out_shape=jax.ShapeDtypeStruct((SENT, rows), jnp.bfloat16),
        in_specs=[ANY] * 4,
        out_specs=VMEM,
        scratch_shapes=[
            pltpu.VMEM((win_dev, SPAN, rows), records.dtype),
            pltpu.VMEM((win_dev, rows), jnp.int32),
            pltpu.VMEM((BINS, BINS), jnp.float32),
            pltpu.VMEM((win_dev, COLS, SPAN), jnp.bfloat16),
            pltpu.SemaphoreType.DMA((2 + 2 * win_dev,)),
        ],
        compiler_params=pltpu.CompilerParams(vmem_limit_bytes=60 * MIB),
        name="whiten",
    )(records.T, validity.T, band_average(), window_tables(win_dev))


def own_kernel(white_hbm, other_ref, out_ref, white_ref, sem):
    copy = pltpu.make_async_copy(white_hbm, white_ref, sem)
    copy.start()
    lanes = pl.ds(pl.multiple_of(place()[0] * 128, 128), 128)
    for half, ref in ((1, other_ref), (0, white_ref)):
        if half == 0:
            copy.wait()
        blocks = [ref[g * COLS : (g + 1) * COLS, lanes].astype(jnp.float32) for g in range(WHITE // COLS)]
        mask = ref[WHITE:SENT, lanes].astype(jnp.float32)
        blocks.append(jnp.concatenate([mask, jnp.zeros((128 - MASK_ROWS, 128), jnp.float32)], axis=0))
        for g, block in enumerate(blocks):
            rows = block.T.astype(jnp.bfloat16)
            at = (half * 2 + g // 2) * CHIP_ROWS
            for x in range(CHIPS):
                piece = rows[x * CHIP_ROWS : (x + 1) * CHIP_ROWS]
                out_ref[x, at : at + CHIP_ROWS, g % 2 * 128 : (g % 2 + 1) * 128] = piece


def own_stations(white, other):
    return pl.pallas_call(
        own_kernel,
        out_shape=jax.ShapeDtypeStruct((CHIPS, OWN, STA), jnp.bfloat16),
        in_specs=[ANY, VMEM],
        out_specs=VMEM,
        scratch_shapes=[pltpu.VMEM((SENT, STA), jnp.bfloat16), pltpu.SemaphoreType.DMA],
        compiler_params=pltpu.CompilerParams(vmem_limit_bytes=4 * MIB),
        name="own",
    )(white, other)


def choose_kernel(partners_ref, *refs):
    blocks, out_ref = refs[:-1], refs[-1]
    for q in range(SLOTS):
        rows = slice(q * SENT, (q + 1) * SENT)
        block, target, _ = partner(partners_ref, q)
        by = jnp.where(target < 0, 0, target - block)

        @pl.when(by == 0)
        def _():
            out_ref[rows] = jnp.zeros((SENT, STA), jnp.bfloat16)

        for step, ref in zip((-1, 1, -2, 2), blocks):

            @pl.when(by == step)
            def _():
                out_ref[rows] = ref[...]


def chosen(partners, blocks):
    return pl.pallas_call(
        choose_kernel,
        out_shape=jax.ShapeDtypeStruct((SLOTS * SENT, STA), jnp.bfloat16),
        in_specs=[SMEM] + [VMEM] * len(blocks),
        out_specs=VMEM,
        compiler_params=pltpu.CompilerParams(vmem_limit_bytes=4 * MIB),
        name="choose",
    )(partners, *blocks)


def turn_kernel(own_ref, lags_hbm, out_ref, mask_ref, held, lag_rows, sem):
    _, chip, core = place()
    copy = pltpu.make_async_copy(lags_hbm, lag_rows, sem)
    copy.start()
    for half in range(2):
        for d, by in enumerate(TURNS):
            source = lax.rem(chip + CHIPS - by, CHIPS)
            for h, whose in enumerate((1 - core, core)):
                here = slice(h * ROW_BLOCK, (h + 1) * ROW_BLOCK)
                for part in range(2):
                    start = pl.multiple_of((half * 2 + part) * CHIP_ROWS + whose * ROW_BLOCK, ROW_BLOCK)
                    rows = own_ref[source, pl.ds(start, ROW_BLOCK)]
                    held[d, here, part * STA : (part + 1) * STA] = rows.astype(jnp.float32)
        mask = held[0, :, WHITE:]
        for d in range(1, CHIPS):
            mask += pltpu.roll(held[d, :, WHITE:], d * MASK_ROWS, 1)
        mask_ref[half] = mask.astype(jnp.bfloat16)
        if half == 0:
            copy.wait()
        cosine, sine = lag_rows[0], lag_rows[1]

        def eight(i, carry):
            stations = pl.ds(pl.multiple_of(i * 8, 8), 8)
            for d in range(CHIPS):
                for g in range(WHITE // COLS):
                    block = held[d, stations, g * COLS : (g + 1) * COLS]
                    swapped = pltpu.roll(block, BINS, 1)
                    lanes = slice(d * WHITE + g * COLS, d * WHITE + (g + 1) * COLS)
                    for k in range(0, 8, 2):
                        turned = [block[m : m + 1] * cosine + swapped[m : m + 1] * sine for m in (k, k + 1)]
                        at = pl.multiple_of(i * TILE + k * LPAD, 2 * LPAD)
                        out_ref[half, pl.ds(at, 2 * LPAD), lanes] = jnp.concatenate(turned, axis=0).astype(jnp.bfloat16)
            return carry

        lax.fori_loop(0, CHIP_ROWS // 8, eight, 0)


def turned_rows(own):
    height = CHIP_ROWS * LPAD
    return pl.pallas_call(
        turn_kernel,
        out_shape=[
            jax.ShapeDtypeStruct((2, height, DEEP), jnp.bfloat16),
            jax.ShapeDtypeStruct((2, CHIP_ROWS, 128), jnp.bfloat16),
        ],
        in_specs=[VMEM, ANY],
        out_specs=[VMEM, VMEM],
        scratch_shapes=[
            pltpu.VMEM((CHIPS, CHIP_ROWS, WIDE), jnp.float32),
            pltpu.VMEM((2, LPAD, COLS), jnp.float32),
            pltpu.SemaphoreType.DMA,
        ],
        compiler_params=pltpu.CompilerParams(vmem_limit_bytes=18 * MIB),
        cost_estimate=pl.CostEstimate(flops=6 * height * DEEP, bytes_accessed=4 * height * DEEP, transcendentals=0),
        name="turn",
    )(own, lag_tables())


def lags_kernel(half, first, count, pieces, has_acc, partners_ref, turned_ref, valid_ref, *refs):
    far = refs[:pieces]
    acc_ref = refs[pieces] if has_acc else None
    out_ref = refs[-1]
    which = [(partner(partners_ref, q)[2] + half) % 2 for q in range(SLOTS)]

    def tile(i, carry):
        source = pl.ds(pl.multiple_of(first * LPAD + i * TILE, TILE), TILE)
        target = pl.ds(pl.multiple_of(i * TILE, TILE), TILE)
        for q in range(SLOTS):
            lanes = slice(q * STA, (q + 1) * STA)
            piece = jnp.concatenate([ref[q * SENT : q * SENT + WHITE] for ref in far], axis=0)
            total = jnp.dot(turned_ref[which[q], source], piece, preferred_element_type=jnp.float32)
            if has_acc:
                total += acc_ref[source, lanes]
            out_ref[target, lanes] = total.astype(out_ref.dtype)
        return carry

    lax.fori_loop(0, count * LPAD // TILE, tile, 0)
    for q in range(SLOTS):
        lanes = slice(q * STA, (q + 1) * STA)
        mask = jnp.concatenate([ref[q * SENT + WHITE : (q + 1) * SENT] for ref in far], axis=0)
        valid = valid_ref[which[q], first : first + count, : CHIPS * MASK_ROWS]
        tally = jnp.dot(valid, mask, preferred_element_type=jnp.float32)
        for m in range(count):
            row = m * LPAD + TALLY_ROW
            value = tally[m : m + 1]
            if has_acc:
                value += acc_ref[first * LPAD + row : first * LPAD + row + 1, lanes]
            out_ref[row : row + 1, lanes] = value.astype(out_ref.dtype)


def into_lags(partners, own, far, half, first, count, acc=None, dtype=jnp.float32):
    args = [partners, *own, *far] + ([] if acc is None else [acc])
    return pl.pallas_call(
        functools.partial(lags_kernel, half, first, count, len(far), acc is not None),
        out_shape=jax.ShapeDtypeStruct((count * LPAD, SLOTS * STA), dtype),
        in_specs=[SMEM] + [VMEM] * (len(args) - 1),
        out_specs=VMEM,
        compiler_params=pltpu.CompilerParams(vmem_limit_bytes=8 * MIB),
        cost_estimate=pl.CostEstimate(
            flops=2 * count * LPAD * SLOTS * STA * DEEP,
            bytes_accessed=4 * count * LPAD * SLOTS * STA,
            transcendentals=0,
        ),
        name="lags",
    )(*args)


def combine_kernel(mine_ref, theirs_ref, out_ref):
    for m in range(out_ref.shape[0]):
        rows = slice(m * LPAD, (m + 1) * LPAD)
        total = mine_ref[rows] + theirs_ref[rows].astype(jnp.float32)
        result = total[:LAGS] / jnp.maximum(total[TALLY_ROW : TALLY_ROW + 1], 1.0)
        for q in range(SLOTS):
            out_ref[m, :, q] = result[:, q * STA : (q + 1) * STA]


def combined(mine, theirs):
    stations = mine.shape[0] // LPAD
    step = 4
    block = pl.BlockSpec((step * LPAD, mine.shape[1]), lambda i: (i, 0))
    out = pl.pallas_call(
        combine_kernel,
        out_shape=jax.ShapeDtypeStruct((stations, LAGS, SLOTS, STA), jnp.float32),
        grid=(stations // step,),
        in_specs=[block, block],
        out_specs=pl.BlockSpec((step, LAGS, SLOTS, STA), lambda i: (i, 0, 0, 0)),
        compiler_params=pltpu.CompilerParams(vmem_limit_bytes=8 * MIB),
        name="combine",
    )(mine, theirs)
    return out.transpose(0, 2, 1, 3)


def body(records, validity, partners):
    partners = partners.T

    def neighbours(white):
        back, on = send(white, to_block(1)), send(white, to_block(-1))
        return [back, on, send(back, to_block(1)), send(on, to_block(-1))]

    def partner_rows(white):
        held = chosen(partners, neighbours(white))
        return [held] + [send(held, to_chip(by)) for by in TURNS[1:]]

    white = whitened(records, validity)
    other = send(white, to_other_half)
    far, other_far = partner_rows(white), partner_rows(other)
    own = own_stations(white, other)
    own = turned_rows(lax.all_to_all(own, "tm", 0, 0, axis_index_groups=CHIP_GROUPS, tiled=True))

    acc = into_lags(partners, own, far, 0, 0, CHIP_ROWS)
    last = functools.partial(into_lags, partners, own, other_far, 1, acc=acc)
    theirs = send(last(0, ROW_BLOCK, dtype=jnp.bfloat16), to_core)
    return combined(last(ROW_BLOCK, ROW_BLOCK), theirs)


def solution(mesh):
    return jax.shard_map(
        body,
        mesh=mesh,
        in_specs=(P("sta", "tm"), P("sta", "tm"), P()),
        out_specs=P(("sta", "tm"), None, None, None),
        check_vma=False,
    )
```

```python
import functools
import math

import jax
import jax.numpy as jnp
import numpy as np
from jax import lax
from jax.experimental import pallas as pl
from jax.experimental.pallas import tpu as pltpu
from jax.sharding import PartitionSpec as P

WIN = 600
BINS = 64
LAG = 32
SLOTS = 2
STA = 256
BLOCKS = 32
TM = 16
HALF = 8
CHIPS = 4
COLS = 2 * BINS
LAGS = 2 * LAG + 1
LPAD = 72
TALLY_ROW = LAGS
MASK_ROWS = 16
ROW_BLOCK = 128 // HALF
CHIP_ROWS = 2 * ROW_BLOCK
WHITE = 3 * COLS
SENT = WHITE + MASK_ROWS
WIDE = WHITE + 128
OWN = 4 * CHIP_ROWS
TURNS = (0, 1, -1, 2)
TILE = 16 * LPAD
DEEP = CHIPS * WHITE
SPAN = 616
AXES = ("sta", "tm")
MIB = 1 << 20


def forward_table():
    sample = np.arange(WIN)
    harmonic = np.arange(1, BINS + 1)
    residue = sample[:, None] * harmonic[None, :] % WIN
    phase = residue.astype(np.float32) * np.float32(2.0 * math.pi / WIN)
    taper = np.float32(0.5) - np.float32(0.5) * np.cos(
        (sample.astype(np.float32) + np.float32(0.5)) * np.float32(2.0 * math.pi / WIN)
    )
    table = np.concatenate([taper[:, None] * np.cos(phase), -taper[:, None] * np.sin(phase)], axis=1)
    return (table * np.float32(1.0 / math.sqrt(WIN))).astype(jnp.bfloat16)


def window_start(w):
    return w * (WIN // 16 * 16)


def window_tables(win_dev):
    table = forward_table()
    out = np.zeros((win_dev, COLS, SPAN), table.dtype)
    for w in range(win_dev):
        at = w * WIN - window_start(w)
        out[w, :, at : at + WIN] = table.T
    return out


def band_average():
    bins = np.arange(BINS)
    nearby = (np.abs(bins[:, None] - bins[None, :]) <= 2).astype(np.float32)
    return np.ascontiguousarray((nearby / nearby.sum(axis=0, keepdims=True)).T)


def routes(target):
    pairs = []
    for b in range(BLOCKS):
        for t in range(TM):
            there = target(b, t)
            if there is not None:
                pairs.append((b * TM + t, there[0] * TM + there[1]))
    return pairs


def to_other_half(b, t):
    return b, (t + HALF) % TM


def to_block(by):
    def target(b, t):
        nb = b + by
        if not 0 <= nb < BLOCKS:
            return None
        return nb, t if nb // 8 == b // 8 else (t + HALF) % TM

    return target


def to_chip(by):
    return lambda b, t: (b, t // HALF * HALF + (t % HALF // 2 + by) % CHIPS * 2 + t % 2)


def to_core(b, t):
    return b, t ^ 1


def send(array, target):
    return lax.ppermute(array, AXES, routes(target))


CHIP_GROUPS = [[z * HALF + 2 * i + c for i in range(CHIPS)] for z in range(TM // HALF) for c in range(2)]


VMEM = pl.BlockSpec(memory_space=pltpu.VMEM)
SMEM = pl.BlockSpec(memory_space=pltpu.SMEM)
ANY = pl.BlockSpec(memory_space=pl.ANY)


def place():
    index = lax.axis_index("tm")
    return index // HALF, index % HALF // 2, index % 2


def partner(partners_ref, q):
    block = lax.axis_index("sta")
    target = partners_ref[q, block]
    return block, target, jnp.where(target // 8 == block // 8, 0, 1)


def whiten_kernel(rec_hbm, mask_hbm, avg_hbm, table_hbm, out_ref, rec, mask_in, avg, table, sems):
    win_dev = table_hbm.shape[0]
    copies = [pltpu.make_async_copy(mask_hbm, mask_in, sems.at[0]), pltpu.make_async_copy(avg_hbm, avg, sems.at[1])]
    for w in range(win_dev):
        copies.append(pltpu.make_async_copy(table_hbm.at[w], table.at[w], sems.at[2 + 2 * w]))
        samples = pl.ds(window_start(w), SPAN)
        copies.append(pltpu.make_async_copy(rec_hbm.at[samples], rec.at[w], sems.at[3 + 2 * w]))
    for copy in copies:
        copy.start()
    copies[0].wait()
    copies[1].wait()
    mask = mask_in[...].astype(jnp.float32)
    for w in range(win_dev):
        copies[2 + 2 * w].wait()
        copies[3 + 2 * w].wait()
        spectra = jnp.dot(table[w], rec[w], preferred_element_type=jnp.float32)
        real, imag = spectra[:BINS], spectra[BINS:]
        power = real * real + imag * imag
        smooth = jnp.dot(avg[...], power, precision=lax.Precision.HIGHEST, preferred_element_type=jnp.float32)
        scale = mask[w : w + 1] / jnp.sqrt(smooth + 0.05)
        out_ref[w * COLS : w * COLS + BINS] = (real * scale).astype(jnp.bfloat16)
        out_ref[w * COLS + BINS : (w + 1) * COLS] = (imag * scale).astype(jnp.bfloat16)
    empty = jnp.zeros((MASK_ROWS - win_dev, STA), jnp.float32)
    out_ref[WHITE:] = jnp.concatenate([mask, empty], axis=0).astype(jnp.bfloat16)


def whitened(records, validity):
    rows, win_dev = validity.shape
    return pl.pallas_call(
        whiten_kernel,
        out_shape=jax.ShapeDtypeStruct((SENT, rows), jnp.bfloat16),
        in_specs=[ANY] * 4,
        out_specs=VMEM,
        scratch_shapes=[
            pltpu.VMEM((win_dev, SPAN, rows), records.dtype),
            pltpu.VMEM((win_dev, rows), jnp.int32),
            pltpu.VMEM((BINS, BINS), jnp.float32),
            pltpu.VMEM((win_dev, COLS, SPAN), jnp.bfloat16),
            pltpu.SemaphoreType.DMA((2 + 2 * win_dev,)),
        ],
        compiler_params=pltpu.CompilerParams(vmem_limit_bytes=60 * MIB),
        name="whiten",
    )(records.T, validity.T, band_average(), window_tables(win_dev))


def rows_kernel(white_ref, out_ref, half=0):
    lanes = pl.ds(pl.multiple_of(place()[0] * 128, 128), 128)
    blocks = [white_ref[g * COLS : (g + 1) * COLS, lanes].astype(jnp.float32) for g in range(WHITE // COLS)]
    mask = white_ref[WHITE:SENT, lanes].astype(jnp.float32)
    blocks.append(jnp.concatenate([mask, jnp.zeros((128 - MASK_ROWS, 128), jnp.float32)], axis=0))
    for g, block in enumerate(blocks):
        rows = block.T.astype(jnp.bfloat16)
        at = (half * 2 + g // 2) * CHIP_ROWS
        for x in range(CHIPS):
            piece = rows[x * CHIP_ROWS : (x + 1) * CHIP_ROWS]
            out_ref[x, at : at + CHIP_ROWS, g % 2 * 128 : (g % 2 + 1) * 128] = piece


def own_kernel(first_ref, other_ref, out_ref):
    out_ref[:, : OWN // 2] = first_ref[...]
    rows_kernel(other_ref, out_ref, 1)


def by_rows(kernel, height, *args):
    return pl.pallas_call(
        kernel,
        out_shape=jax.ShapeDtypeStruct((CHIPS, height, STA), jnp.bfloat16),
        in_specs=[VMEM] * len(args),
        out_specs=VMEM,
        compiler_params=pltpu.CompilerParams(vmem_limit_bytes=4 * MIB),
        name="rows",
    )(*args)


def choose_kernel(partners_ref, *refs):
    blocks, out_ref = refs[:-1], refs[-1]
    for q in range(SLOTS):
        rows = slice(q * SENT, (q + 1) * SENT)
        block, target, _ = partner(partners_ref, q)
        by = jnp.where(target < 0, 0, target - block)

        @pl.when(by == 0)
        def _():
            out_ref[rows] = jnp.zeros((SENT, STA), jnp.bfloat16)

        for step, ref in zip((-1, 1, -2, 2), blocks):

            @pl.when(by == step)
            def _():
                out_ref[rows] = ref[...]


def chosen(partners, blocks):
    return pl.pallas_call(
        choose_kernel,
        out_shape=jax.ShapeDtypeStruct((SLOTS * SENT, STA), jnp.bfloat16),
        in_specs=[SMEM] + [VMEM] * len(blocks),
        out_specs=VMEM,
        compiler_params=pltpu.CompilerParams(vmem_limit_bytes=4 * MIB),
        name="choose",
    )(partners, *blocks)


def lag_tables():
    lag = lax.broadcasted_iota(jnp.int32, (LPAD, COLS), 0) - LAG
    column = lax.broadcasted_iota(jnp.int32, (LPAD, COLS), 1)
    harmonic = jnp.where(column < BINS, column, column - BINS) + 1
    turns = (lag * harmonic).astype(jnp.float32) * (1.0 / WIN)
    phase = (turns - jnp.round(turns)) * (2.0 * math.pi)
    kept = lag <= LAG
    sine = jnp.where(column < BINS, -jnp.sin(phase), jnp.sin(phase))
    return jnp.where(kept, jnp.cos(phase), 0.0), jnp.where(kept, sine, 0.0)


def turn_kernel(own_ref, out_ref, mask_ref, held):
    _, chip, core = place()
    cosine, sine = lag_tables()
    for half in range(2):
        for d, by in enumerate(TURNS):
            source = lax.rem(chip + CHIPS - by, CHIPS)
            for h, whose in enumerate((1 - core, core)):
                here = slice(h * ROW_BLOCK, (h + 1) * ROW_BLOCK)
                for part in range(2):
                    start = pl.multiple_of((half * 2 + part) * CHIP_ROWS + whose * ROW_BLOCK, ROW_BLOCK)
                    rows = own_ref[source, pl.ds(start, ROW_BLOCK)]
                    held[d, here, part * STA : (part + 1) * STA] = rows.astype(jnp.float32)
        mask = held[0, :, WHITE:]
        for d in range(1, CHIPS):
            mask += pltpu.roll(held[d, :, WHITE:], d * MASK_ROWS, 1)
        mask_ref[half] = mask.astype(jnp.bfloat16)

        def eight(i, carry):
            stations = pl.ds(pl.multiple_of(i * 8, 8), 8)
            for d in range(CHIPS):
                for g in range(WHITE // COLS):
                    block = held[d, stations, g * COLS : (g + 1) * COLS]
                    swapped = pltpu.roll(block, BINS, 1)
                    lanes = slice(d * WHITE + g * COLS, d * WHITE + (g + 1) * COLS)
                    for k in range(0, 8, 2):
                        turned = [block[m : m + 1] * cosine + swapped[m : m + 1] * sine for m in (k, k + 1)]
                        at = pl.multiple_of(i * 8 * LPAD + k * LPAD, 2 * LPAD)
                        out_ref[half, pl.ds(at, 2 * LPAD), lanes] = jnp.concatenate(turned, axis=0).astype(jnp.bfloat16)
            return carry

        lax.fori_loop(0, CHIP_ROWS // 8, eight, 0)


def turned_rows(own):
    height = CHIP_ROWS * LPAD
    return pl.pallas_call(
        turn_kernel,
        out_shape=[
            jax.ShapeDtypeStruct((2, height, DEEP), jnp.bfloat16),
            jax.ShapeDtypeStruct((2, CHIP_ROWS, 128), jnp.bfloat16),
        ],
        in_specs=[VMEM],
        out_specs=[VMEM, VMEM],
        scratch_shapes=[pltpu.VMEM((CHIPS, CHIP_ROWS, WIDE), jnp.float32)],
        compiler_params=pltpu.CompilerParams(vmem_limit_bytes=18 * MIB),
        cost_estimate=pl.CostEstimate(flops=6 * height * DEEP, bytes_accessed=4 * height * DEEP, transcendentals=0),
        name="turn",
    )(own)


def lags_kernel(groups, first, count, has_acc, partners_ref, turned_ref, valid_ref, *refs):
    acc_ref = refs[-2] if has_acc else None
    out_ref = refs[-1]
    taken, at = [], 0
    for half, low, high in groups:
        taken.append((half, low, high, refs[at : at + high - low]))
        at += high - low

    def half_of(q, half):
        return (partner(partners_ref, q)[2] + half) % 2

    def tile(i, carry):
        source = pl.ds(pl.multiple_of(first * LPAD + i * TILE, TILE), TILE)
        target = pl.ds(pl.multiple_of(i * TILE, TILE), TILE)
        for q in range(SLOTS):
            lanes = slice(q * STA, (q + 1) * STA)
            total = acc_ref[source, lanes] if has_acc else 0.0
            for half, low, high, far in taken:
                rows = jnp.concatenate([ref[q * SENT : q * SENT + WHITE] for ref in far], axis=0)
                turned = turned_ref[half_of(q, half), source, low * WHITE : high * WHITE]
                total += jnp.dot(turned, rows, preferred_element_type=jnp.float32)
            out_ref[target, lanes] = total.astype(out_ref.dtype)
        return carry

    lax.fori_loop(0, count * LPAD // TILE, tile, 0)
    for q in range(SLOTS):
        lanes = slice(q * STA, (q + 1) * STA)
        tally = 0.0
        for half, low, high, far in taken:
            mask = jnp.concatenate([ref[q * SENT + WHITE : (q + 1) * SENT] for ref in far], axis=0)
            valid = valid_ref[half_of(q, half), first : first + count]
            valid = valid[:, low * MASK_ROWS : high * MASK_ROWS]
            tally += jnp.dot(valid, mask, preferred_element_type=jnp.float32)
        for m in range(count):
            row = m * LPAD + TALLY_ROW
            value = tally[m : m + 1]
            if has_acc:
                value += acc_ref[first * LPAD + row : first * LPAD + row + 1, lanes]
            out_ref[row : row + 1, lanes] = value.astype(out_ref.dtype)


def into_lags(partners, own, groups, first, count, acc=None, dtype=jnp.float32):
    far = [piece for _, _, pieces in groups for piece in pieces]
    args = [partners, *own, *far] + ([] if acc is None else [acc])
    spans = tuple((half, low, low + len(pieces)) for half, low, pieces in groups)
    return pl.pallas_call(
        functools.partial(lags_kernel, spans, first, count, acc is not None),
        out_shape=jax.ShapeDtypeStruct((count * LPAD, SLOTS * STA), dtype),
        in_specs=[SMEM] + [VMEM] * (len(args) - 1),
        out_specs=VMEM,
        compiler_params=pltpu.CompilerParams(vmem_limit_bytes=8 * MIB),
        cost_estimate=pl.CostEstimate(
            flops=2 * count * LPAD * SLOTS * STA * WHITE * len(far),
            bytes_accessed=4 * count * LPAD * SLOTS * STA,
            transcendentals=0,
        ),
        name="lags",
    )(*args)


def combine_kernel(mine_ref, theirs_ref, out_hbm, out, sems):
    parts = sems.shape[0]
    step = out.shape[0] // parts
    copies = []
    for i in range(parts):
        for m in range(i * step, (i + 1) * step):
            rows = slice(m * LPAD, (m + 1) * LPAD)
            total = mine_ref[rows] + theirs_ref[rows].astype(jnp.float32)
            result = total[:LAGS] / jnp.maximum(total[TALLY_ROW : TALLY_ROW + 1], 1.0)
            for q in range(SLOTS):
                out[m, :, q] = result[:, q * STA : (q + 1) * STA]
        here = pl.ds(i * step, step)
        copies.append(pltpu.make_async_copy(out.at[here], out_hbm.at[here], sems.at[i]))
        copies[-1].start()
    for copy in copies:
        copy.wait()


def combined(mine, theirs):
    shape = (mine.shape[0] // LPAD, LAGS, SLOTS, STA)
    out = pl.pallas_call(
        combine_kernel,
        out_shape=jax.ShapeDtypeStruct(shape, jnp.float32),
        in_specs=[VMEM, VMEM],
        out_specs=ANY,
        scratch_shapes=[pltpu.VMEM(shape, jnp.float32), pltpu.SemaphoreType.DMA((8,))],
        compiler_params=pltpu.CompilerParams(vmem_limit_bytes=8 * MIB),
        name="combine",
    )(mine, theirs)
    return out.transpose(0, 2, 1, 3)


def body(records, validity, partners):
    partners = partners.T

    def neighbours(white):
        back, on = send(white, to_block(1)), send(white, to_block(-1))
        return [back, on, send(back, to_block(1)), send(on, to_block(-1))]

    def spread(held):
        return [held] + [send(held, to_chip(by)) for by in TURNS[1:]]

    white = whitened(records, validity)
    other = send(white, to_other_half)
    rows = by_rows(rows_kernel, OWN // 2, white)
    rows, other = lax.optimization_barrier((rows, other))
    far, other_far = spread(chosen(partners, neighbours(white))), spread(chosen(partners, neighbours(other)))
    own = by_rows(own_kernel, OWN, rows, other)
    own = turned_rows(lax.all_to_all(own, "tm", 0, 0, axis_index_groups=CHIP_GROUPS, tiled=True))

    acc = into_lags(partners, own, [(0, 0, far)], 0, CHIP_ROWS)
    last = functools.partial(into_lags, partners, own, [(1, 0, other_far)], acc=acc)
    theirs = send(last(0, ROW_BLOCK, dtype=jnp.bfloat16), to_core)
    return combined(last(ROW_BLOCK, ROW_BLOCK), theirs)


def solution(mesh):
    return jax.shard_map(
        body,
        mesh=mesh,
        in_specs=(P("sta", "tm"), P("sta", "tm"), P()),
        out_specs=P(("sta", "tm"), None, None, None),
        check_vma=False,
    )
```

```python
import functools
import math

import jax
import jax.numpy as jnp
import numpy as np
from jax import lax
from jax.experimental import pallas as pl
from jax.experimental.pallas import tpu as pltpu
from jax.sharding import PartitionSpec as P

WIN = 600
BINS = 64
LAG = 32
SLOTS = 2
STA = 256
BLOCKS = 32
TM = 16
HALF = 8
CHIPS = 4
COLS = 2 * BINS
LAGS = 2 * LAG + 1
LPAD = 72
TALLY_ROW = LAGS
MASK_ROWS = 16
ROW_BLOCK = 128 // HALF
CHIP_ROWS = 2 * ROW_BLOCK
WHITE = 3 * COLS
SENT = WHITE + MASK_ROWS
WIDE = WHITE + 128
OWN_AT = SLOTS * SENT
OWN = 4 * CHIP_ROWS
TURNS = (0, 1, -1, 2)
TILE = 16 * LPAD
DEEP = CHIPS * WHITE
SPAN = 616
AXES = ("sta", "tm")
MIB = 1 << 20


def forward_table():
    sample = np.arange(WIN)
    harmonic = np.arange(1, BINS + 1)
    residue = sample[:, None] * harmonic[None, :] % WIN
    phase = residue.astype(np.float32) * np.float32(2.0 * math.pi / WIN)
    taper = np.float32(0.5) - np.float32(0.5) * np.cos(
        (sample.astype(np.float32) + np.float32(0.5)) * np.float32(2.0 * math.pi / WIN)
    )
    table = np.concatenate([taper[:, None] * np.cos(phase), -taper[:, None] * np.sin(phase)], axis=1)
    return (table * np.float32(1.0 / math.sqrt(WIN))).astype(jnp.bfloat16)


def window_start(w):
    return w * (WIN // 16 * 16)


def window_tables(win_dev):
    table = forward_table()
    out = np.zeros((win_dev, COLS, SPAN), table.dtype)
    for w in range(win_dev):
        at = w * WIN - window_start(w)
        out[w, :, at : at + WIN] = table.T
    return out


def band_average():
    bins = np.arange(BINS)
    nearby = (np.abs(bins[:, None] - bins[None, :]) <= 2).astype(np.float32)
    return np.ascontiguousarray((nearby / nearby.sum(axis=0, keepdims=True)).T)


def routes(target):
    pairs = []
    for b in range(BLOCKS):
        for t in range(TM):
            there = target(b, t)
            if there is not None:
                pairs.append((b * TM + t, there[0] * TM + there[1]))
    return pairs


def to_other_half(b, t):
    return b, (t + HALF) % TM


def to_block(by):
    def target(b, t):
        nb = b + by
        if not 0 <= nb < BLOCKS:
            return None
        return nb, t if nb // 8 == b // 8 else (t + HALF) % TM

    return target


def to_chip(by):
    return lambda b, t: (b, t // HALF * HALF + (t % HALF // 2 + by) % CHIPS * 2 + t % 2)


def to_core(b, t):
    return b, t ^ 1


def send(array, target):
    return lax.ppermute(array, AXES, routes(target))


CHIP_GROUPS = [[z * HALF + 2 * i + c for i in range(CHIPS)] for z in range(TM // HALF) for c in range(2)]


VMEM = pl.BlockSpec(memory_space=pltpu.VMEM)
SMEM = pl.BlockSpec(memory_space=pltpu.SMEM)
ANY = pl.BlockSpec(memory_space=pl.ANY)


def place():
    index = lax.axis_index("tm")
    return index // HALF, index % HALF // 2, index % 2


def partner(partners_ref, q):
    block = lax.axis_index("sta")
    target = partners_ref[q, block]
    return block, target, jnp.where(target // 8 == block // 8, 0, 1)


def whiten_kernel(rec_hbm, mask_hbm, avg_hbm, table_hbm, out_ref, rec, mask_in, avg, table, sems):
    win_dev = table_hbm.shape[0]
    copies = [pltpu.make_async_copy(mask_hbm, mask_in, sems.at[0]), pltpu.make_async_copy(avg_hbm, avg, sems.at[1])]
    for w in range(win_dev):
        copies.append(pltpu.make_async_copy(table_hbm.at[w], table.at[w], sems.at[2 + 2 * w]))
        samples = pl.ds(window_start(w), SPAN)
        copies.append(pltpu.make_async_copy(rec_hbm.at[samples], rec.at[w], sems.at[3 + 2 * w]))
    for copy in copies:
        copy.start()
    copies[0].wait()
    copies[1].wait()
    mask = mask_in[...].astype(jnp.float32)
    for w in range(win_dev):
        copies[2 + 2 * w].wait()
        copies[3 + 2 * w].wait()
        spectra = jnp.dot(table[w], rec[w], preferred_element_type=jnp.float32)
        real, imag = spectra[:BINS], spectra[BINS:]
        power = real * real + imag * imag
        smooth = jnp.dot(avg[...], power, precision=lax.Precision.HIGHEST, preferred_element_type=jnp.float32)
        scale = mask[w : w + 1] / jnp.sqrt(smooth + 0.05)
        out_ref[w * COLS : w * COLS + BINS] = (real * scale).astype(jnp.bfloat16)
        out_ref[w * COLS + BINS : (w + 1) * COLS] = (imag * scale).astype(jnp.bfloat16)
    empty = jnp.zeros((MASK_ROWS - win_dev, STA), jnp.float32)
    out_ref[WHITE:] = jnp.concatenate([mask, empty], axis=0).astype(jnp.bfloat16)


def whitened(records, validity):
    rows, win_dev = validity.shape
    return pl.pallas_call(
        whiten_kernel,
        out_shape=jax.ShapeDtypeStruct((SENT, rows), jnp.bfloat16),
        in_specs=[ANY] * 4,
        out_specs=VMEM,
        scratch_shapes=[
            pltpu.VMEM((win_dev, SPAN, rows), records.dtype),
            pltpu.VMEM((win_dev, rows), jnp.int32),
            pltpu.VMEM((BINS, BINS), jnp.float32),
            pltpu.VMEM((win_dev, COLS, SPAN), jnp.bfloat16),
            pltpu.SemaphoreType.DMA((2 + 2 * win_dev,)),
        ],
        compiler_params=pltpu.CompilerParams(vmem_limit_bytes=60 * MIB),
        name="whiten",
    )(records.T, validity.T, band_average(), window_tables(win_dev))


def store_rows(out_ref, white_ref, at):
    lanes = pl.ds(pl.multiple_of(place()[0] * 128, 128), 128)
    blocks = [white_ref[g * COLS : (g + 1) * COLS, lanes].astype(jnp.float32) for g in range(WHITE // COLS)]
    mask = white_ref[WHITE:SENT, lanes].astype(jnp.float32)
    blocks.append(jnp.concatenate([mask, jnp.zeros((128 - MASK_ROWS, 128), jnp.float32)], axis=0))
    for g, block in enumerate(blocks):
        rows = block.T.astype(jnp.bfloat16)
        here = slice(at + g // 2 * CHIP_ROWS, at + (g // 2 + 1) * CHIP_ROWS)
        for x in range(CHIPS):
            piece = rows[x * CHIP_ROWS : (x + 1) * CHIP_ROWS]
            out_ref[x, here, g % 2 * 128 : (g % 2 + 1) * 128] = piece


def rows_kernel(partners_ref, white_ref, out_ref):
    del partners_ref
    store_rows(out_ref, white_ref, 0)


def own_rows(partners, white):
    return pl.pallas_call(
        rows_kernel,
        out_shape=jax.ShapeDtypeStruct((CHIPS, OWN // 2, STA), jnp.bfloat16),
        in_specs=[SMEM, VMEM],
        out_specs=VMEM,
        compiler_params=pltpu.CompilerParams(vmem_limit_bytes=4 * MIB),
        name="rows",
    )(partners, white)


def choose_kernel(partners_ref, *refs):
    blocks, own, out_ref = refs[:4], refs[4:-1], refs[-1]
    if own:
        rows_ref, other_ref = own
        out_ref[:, OWN_AT : OWN_AT + OWN // 2] = rows_ref[...]
        store_rows(out_ref, other_ref, OWN_AT + OWN // 2)
    for q in range(SLOTS):
        here = slice(q * SENT, (q + 1) * SENT)
        block, target, _ = partner(partners_ref, q)
        by = jnp.where(target < 0, 0, target - block)

        @pl.when(by == 0)
        def _():
            for x in range(out_ref.shape[0]):
                out_ref[x, here] = jnp.zeros((SENT, STA), jnp.bfloat16)

        for step, ref in zip((-1, 1, -2, 2), blocks):

            @pl.when(by == step)
            def _():
                for x in range(out_ref.shape[0]):
                    out_ref[x, here] = ref[...]


def chosen(partners, blocks, *own):
    shape = (CHIPS, OWN_AT + OWN, STA) if own else (1, OWN_AT, STA)
    return pl.pallas_call(
        choose_kernel,
        out_shape=jax.ShapeDtypeStruct(shape, jnp.bfloat16),
        in_specs=[SMEM] + [VMEM] * (len(blocks) + len(own)),
        out_specs=VMEM,
        compiler_params=pltpu.CompilerParams(vmem_limit_bytes=4 * MIB),
        name="choose",
    )(partners, *blocks, *own)


def lag_tables():
    lag = lax.broadcasted_iota(jnp.int32, (LPAD, COLS), 0) - LAG
    column = lax.broadcasted_iota(jnp.int32, (LPAD, COLS), 1)
    harmonic = jnp.where(column < BINS, column, column - BINS) + 1
    turns = (lag * harmonic).astype(jnp.float32) * (1.0 / WIN)
    phase = (turns - jnp.round(turns)) * (2.0 * math.pi)
    kept = lag <= LAG
    sine = jnp.where(column < BINS, -jnp.sin(phase), jnp.sin(phase))
    return jnp.where(kept, jnp.cos(phase), 0.0), jnp.where(kept, sine, 0.0)


def turn_kernel(own_ref, out_ref, mask_ref, held):
    _, chip, core = place()
    cosine, sine = lag_tables()
    for half in range(2):
        for d, by in enumerate(TURNS):
            source = lax.rem(chip + CHIPS - by, CHIPS)
            for h, whose in enumerate((1 - core, core)):
                here = slice(h * ROW_BLOCK, (h + 1) * ROW_BLOCK)
                for part in range(2):
                    at = OWN_AT + (half * 2 + part) * CHIP_ROWS
                    start = pl.multiple_of(at + whose * ROW_BLOCK, ROW_BLOCK)
                    rows = own_ref[source, pl.ds(start, ROW_BLOCK)]
                    held[d, here, part * STA : (part + 1) * STA] = rows.astype(jnp.float32)
        mask = held[0, :, WHITE:]
        for d in range(1, CHIPS):
            mask += pltpu.roll(held[d, :, WHITE:], d * MASK_ROWS, 1)
        mask_ref[half] = mask.astype(jnp.bfloat16)

        def eight(i, carry):
            stations = pl.ds(pl.multiple_of(i * 8, 8), 8)
            for d in range(CHIPS):
                for g in range(WHITE // COLS):
                    block = held[d, stations, g * COLS : (g + 1) * COLS]
                    swapped = pltpu.roll(block, BINS, 1)
                    lanes = slice(d * WHITE + g * COLS, d * WHITE + (g + 1) * COLS)
                    for k in range(0, 8, 2):
                        turned = [block[m : m + 1] * cosine + swapped[m : m + 1] * sine for m in (k, k + 1)]
                        at = pl.multiple_of(i * 8 * LPAD + k * LPAD, 2 * LPAD)
                        out_ref[half, pl.ds(at, 2 * LPAD), lanes] = jnp.concatenate(turned, axis=0).astype(jnp.bfloat16)
            return carry

        lax.fori_loop(0, CHIP_ROWS // 8, eight, 0)


def turned_rows(own):
    height = CHIP_ROWS * LPAD
    return pl.pallas_call(
        turn_kernel,
        out_shape=[
            jax.ShapeDtypeStruct((2, height, DEEP), jnp.bfloat16),
            jax.ShapeDtypeStruct((2, CHIP_ROWS, 128), jnp.bfloat16),
        ],
        in_specs=[VMEM],
        out_specs=[VMEM, VMEM],
        scratch_shapes=[pltpu.VMEM((CHIPS, CHIP_ROWS, WIDE), jnp.float32)],
        compiler_params=pltpu.CompilerParams(vmem_limit_bytes=18 * MIB),
        cost_estimate=pl.CostEstimate(flops=6 * height * DEEP, bytes_accessed=4 * height * DEEP, transcendentals=0),
        name="turn",
    )(own)


def lags_kernel(groups, first, count, has_acc, partners_ref, turned_ref, valid_ref, *refs):
    acc_ref = refs[-2] if has_acc else None
    out_ref = refs[-1]
    taken, at = [], 0
    for half, low, high, gathered in groups:
        if gathered:
            chip = place()[1]
            taken.append((half, low, high, [refs[at].at[lax.rem(chip + CHIPS - by, CHIPS)] for by in TURNS]))
            at += 1
        else:
            taken.append((half, low, high, refs[at : at + high - low]))
            at += high - low

    def half_of(q, half):
        return (partner(partners_ref, q)[2] + half) % 2

    def tile(i, carry):
        source = pl.ds(pl.multiple_of(first * LPAD + i * TILE, TILE), TILE)
        target = pl.ds(pl.multiple_of(i * TILE, TILE), TILE)
        for q in range(SLOTS):
            lanes = slice(q * STA, (q + 1) * STA)
            total = acc_ref[source, lanes] if has_acc else 0.0
            for half, low, high, far in taken:
                rows = jnp.concatenate([ref[q * SENT : q * SENT + WHITE] for ref in far], axis=0)
                turned = turned_ref[half_of(q, half), source, low * WHITE : high * WHITE]
                total += jnp.dot(turned, rows, preferred_element_type=jnp.float32)
            out_ref[target, lanes] = total.astype(out_ref.dtype)
        return carry

    lax.fori_loop(0, count * LPAD // TILE, tile, 0)
    for q in range(SLOTS):
        lanes = slice(q * STA, (q + 1) * STA)
        tally = 0.0
        for half, low, high, far in taken:
            mask = jnp.concatenate([ref[q * SENT + WHITE : (q + 1) * SENT] for ref in far], axis=0)
            valid = valid_ref[half_of(q, half), first : first + count]
            valid = valid[:, low * MASK_ROWS : high * MASK_ROWS]
            tally += jnp.dot(valid, mask, preferred_element_type=jnp.float32)
        for m in range(count):
            row = m * LPAD + TALLY_ROW
            value = tally[m : m + 1]
            if has_acc:
                value += acc_ref[first * LPAD + row : first * LPAD + row + 1, lanes]
            out_ref[row : row + 1, lanes] = value.astype(out_ref.dtype)


def into_lags(partners, own, groups, first, count, acc=None, dtype=jnp.float32):
    far = [piece for _, _, pieces in groups for piece in pieces]
    args = [partners, *own, *far] + ([] if acc is None else [acc])
    spans = tuple(
        (half, low, CHIPS if pieces[0].ndim == 3 else low + len(pieces), pieces[0].ndim == 3)
        for half, low, pieces in groups
    )
    return pl.pallas_call(
        functools.partial(lags_kernel, spans, first, count, acc is not None),
        out_shape=jax.ShapeDtypeStruct((count * LPAD, SLOTS * STA), dtype),
        in_specs=[SMEM] + [VMEM] * (len(args) - 1),
        out_specs=VMEM,
        compiler_params=pltpu.CompilerParams(vmem_limit_bytes=8 * MIB),
        cost_estimate=pl.CostEstimate(
            flops=2 * count * LPAD * SLOTS * STA * WHITE * len(far),
            bytes_accessed=4 * count * LPAD * SLOTS * STA,
            transcendentals=0,
        ),
        name="lags",
    )(*args)


def combine_kernel(mine_ref, theirs_ref, out_hbm, out, sems):
    parts = sems.shape[0]
    step = out.shape[0] // parts
    copies = []
    for i in range(parts):
        for m in range(i * step, (i + 1) * step):
            rows = slice(m * LPAD, (m + 1) * LPAD)
            total = mine_ref[rows] + theirs_ref[rows].astype(jnp.float32)
            result = total[:LAGS] / jnp.maximum(total[TALLY_ROW : TALLY_ROW + 1], 1.0)
            for q in range(SLOTS):
                out[m, :, q] = result[:, q * STA : (q + 1) * STA]
        here = pl.ds(i * step, step)
        copies.append(pltpu.make_async_copy(out.at[here], out_hbm.at[here], sems.at[i]))
        copies[-1].start()
    for copy in copies:
        copy.wait()


def combined(mine, theirs):
    shape = (mine.shape[0] // LPAD, LAGS, SLOTS, STA)
    out = pl.pallas_call(
        combine_kernel,
        out_shape=jax.ShapeDtypeStruct(shape, jnp.float32),
        in_specs=[VMEM, VMEM],
        out_specs=ANY,
        scratch_shapes=[pltpu.VMEM(shape, jnp.float32), pltpu.SemaphoreType.DMA((8,))],
        compiler_params=pltpu.CompilerParams(vmem_limit_bytes=8 * MIB),
        name="combine",
    )(mine, theirs)
    return out.transpose(0, 2, 1, 3)


def body(records, validity, partners):
    partners = partners.T

    def neighbours(white):
        back, on = send(white, to_block(1)), send(white, to_block(-1))
        return [back, on, send(back, to_block(1)), send(on, to_block(-1))]

    def to_chips(array):
        return lax.all_to_all(array, "tm", 0, 0, axis_index_groups=CHIP_GROUPS, tiled=True)

    white = whitened(records, validity)
    other = send(white, to_other_half)
    rows, other = lax.optimization_barrier((own_rows(partners, white), other))
    near = neighbours(white)
    other_near = neighbours(other)
    near[2], near[3], late = lax.optimization_barrier((near[2], near[3], other))
    far = to_chips(chosen(partners, near, rows, late))
    (held,) = chosen(partners, other_near)
    other_far = [held] + [send(held, to_chip(by)) for by in TURNS[1:]]
    own = turned_rows(far)

    acc = into_lags(partners, own, [(0, 0, [far]), (1, 0, other_far[:1])], 0, CHIP_ROWS)
    last = functools.partial(into_lags, partners, own, [(1, 1, other_far[1:])], acc=acc)
    theirs = send(last(0, ROW_BLOCK, dtype=jnp.bfloat16), to_core)
    return combined(last(ROW_BLOCK, ROW_BLOCK), theirs)


def solution(mesh):
    return jax.shard_map(
        body,
        mesh=mesh,
        in_specs=(P("sta", "tm"), P("sta", "tm"), P()),
        out_specs=P(("sta", "tm"), None, None, None),
        check_vma=False,
    )
```

```python
import functools
import math

import jax
import jax.numpy as jnp
import numpy as np
from jax import lax
from jax.experimental import pallas as pl
from jax.experimental.pallas import tpu as pltpu
from jax.sharding import PartitionSpec as P

WIN = 600
BINS = 64
LAG = 32
SLOTS = 2
STA = 256
BLOCKS = 32
TM = 16
HALF = 8
CHIPS = 4
COLS = 2 * BINS
LAGS = 2 * LAG + 1
LPAD = 72
TALLY_ROW = LAGS
MASK_ROWS = 16
ROW_BLOCK = 128 // HALF
CHIP_ROWS = 2 * ROW_BLOCK
WHITE = 3 * COLS
SENT = WHITE + MASK_ROWS
WIDE = WHITE + 128
OWN = 4 * CHIP_ROWS
TURNS = (0, 1, -1, 2)
TILE = 16 * LPAD
DEEP = CHIPS * WHITE
SPAN = 616
AXES = ("sta", "tm")
MIB = 1 << 20


def forward_table():
    sample = np.arange(WIN)
    harmonic = np.arange(1, BINS + 1)
    residue = sample[:, None] * harmonic[None, :] % WIN
    phase = residue.astype(np.float32) * np.float32(2.0 * math.pi / WIN)
    taper = np.float32(0.5) - np.float32(0.5) * np.cos(
        (sample.astype(np.float32) + np.float32(0.5)) * np.float32(2.0 * math.pi / WIN)
    )
    table = np.concatenate([taper[:, None] * np.cos(phase), -taper[:, None] * np.sin(phase)], axis=1)
    return (table * np.float32(1.0 / math.sqrt(WIN))).astype(jnp.bfloat16)


def window_start(w):
    return w * (WIN // 16 * 16)


def window_tables(win_dev):
    table = forward_table()
    out = np.zeros((win_dev, COLS, SPAN), table.dtype)
    for w in range(win_dev):
        at = w * WIN - window_start(w)
        out[w, :, at : at + WIN] = table.T
    return out


def band_average():
    bins = np.arange(BINS)
    nearby = (np.abs(bins[:, None] - bins[None, :]) <= 2).astype(np.float32)
    return np.ascontiguousarray((nearby / nearby.sum(axis=0, keepdims=True)).T)


def routes(target):
    pairs = []
    for b in range(BLOCKS):
        for t in range(TM):
            there = target(b, t)
            if there is not None:
                pairs.append((b * TM + t, there[0] * TM + there[1]))
    return pairs


def to_other_half(b, t):
    return b, (t + HALF) % TM


def to_block(by):
    def target(b, t):
        nb = b + by
        if not 0 <= nb < BLOCKS:
            return None
        return nb, t if nb // 8 == b // 8 else (t + HALF) % TM

    return target


def to_chip(by):
    return lambda b, t: (b, t // HALF * HALF + (t % HALF // 2 + by) % CHIPS * 2 + t % 2)


def to_core(b, t):
    return b, t ^ 1


def send(array, target):
    return lax.ppermute(array, AXES, routes(target))


CHIP_GROUPS = [[z * HALF + 2 * i + c for i in range(CHIPS)] for z in range(TM // HALF) for c in range(2)]


VMEM = pl.BlockSpec(memory_space=pltpu.VMEM)
SMEM = pl.BlockSpec(memory_space=pltpu.SMEM)
ANY = pl.BlockSpec(memory_space=pl.ANY)


def place():
    index = lax.axis_index("tm")
    return index // HALF, index % HALF // 2, index % 2


def partner(partners_ref, q):
    block = lax.axis_index("sta")
    target = partners_ref[q, block]
    return block, target, jnp.where(target // 8 == block // 8, 0, 1)


def whiten_kernel(rec_hbm, mask_hbm, avg_hbm, table_hbm, out_ref, rec, mask_in, avg, table, sems):
    win_dev = table_hbm.shape[0]
    copies = [pltpu.make_async_copy(mask_hbm, mask_in, sems.at[0]), pltpu.make_async_copy(avg_hbm, avg, sems.at[1])]
    for w in range(win_dev):
        copies.append(pltpu.make_async_copy(table_hbm.at[w], table.at[w], sems.at[2 + 2 * w]))
        samples = pl.ds(window_start(w), SPAN)
        copies.append(pltpu.make_async_copy(rec_hbm.at[samples], rec.at[w], sems.at[3 + 2 * w]))
    for copy in copies:
        copy.start()
    copies[0].wait()
    copies[1].wait()
    mask = mask_in[...].astype(jnp.float32)
    for w in range(win_dev):
        copies[2 + 2 * w].wait()
        copies[3 + 2 * w].wait()
        spectra = jnp.dot(table[w], rec[w], preferred_element_type=jnp.float32)
        real, imag = spectra[:BINS], spectra[BINS:]
        power = real * real + imag * imag
        smooth = jnp.dot(avg[...], power, precision=lax.Precision.HIGHEST, preferred_element_type=jnp.float32)
        scale = mask[w : w + 1] / jnp.sqrt(smooth + 0.05)
        out_ref[w * COLS : w * COLS + BINS] = (real * scale).astype(jnp.bfloat16)
        out_ref[w * COLS + BINS : (w + 1) * COLS] = (imag * scale).astype(jnp.bfloat16)
    empty = jnp.zeros((MASK_ROWS - win_dev, STA), jnp.float32)
    out_ref[WHITE:] = jnp.concatenate([mask, empty], axis=0).astype(jnp.bfloat16)


def whitened(records, validity):
    rows, win_dev = validity.shape
    return pl.pallas_call(
        whiten_kernel,
        out_shape=jax.ShapeDtypeStruct((SENT, rows), jnp.bfloat16),
        in_specs=[ANY] * 4,
        out_specs=VMEM,
        scratch_shapes=[
            pltpu.VMEM((win_dev, SPAN, rows), records.dtype),
            pltpu.VMEM((win_dev, rows), jnp.int32),
            pltpu.VMEM((BINS, BINS), jnp.float32),
            pltpu.VMEM((win_dev, COLS, SPAN), jnp.bfloat16),
            pltpu.SemaphoreType.DMA((2 + 2 * win_dev,)),
        ],
        compiler_params=pltpu.CompilerParams(vmem_limit_bytes=60 * MIB),
        name="whiten",
    )(records.T, validity.T, band_average(), window_tables(win_dev))


def first_rows_kernel(partners_ref, white_ref, out_ref):
    del partners_ref
    rows_kernel(white_ref, out_ref)


def rows_kernel(white_ref, out_ref, half=0):
    lanes = pl.ds(pl.multiple_of(place()[0] * 128, 128), 128)
    blocks = [white_ref[g * COLS : (g + 1) * COLS, lanes].astype(jnp.float32) for g in range(WHITE // COLS)]
    mask = white_ref[WHITE:SENT, lanes].astype(jnp.float32)
    blocks.append(jnp.concatenate([mask, jnp.zeros((128 - MASK_ROWS, 128), jnp.float32)], axis=0))
    for g, block in enumerate(blocks):
        rows = block.T.astype(jnp.bfloat16)
        at = (half * 2 + g // 2) * CHIP_ROWS
        for x in range(CHIPS):
            piece = rows[x * CHIP_ROWS : (x + 1) * CHIP_ROWS]
            out_ref[x, at : at + CHIP_ROWS, g % 2 * 128 : (g % 2 + 1) * 128] = piece


def own_kernel(first_ref, other_ref, out_ref):
    out_ref[:, : OWN // 2] = first_ref[...]
    rows_kernel(other_ref, out_ref, 1)


def by_rows(kernel, height, *args):
    return pl.pallas_call(
        kernel,
        out_shape=jax.ShapeDtypeStruct((CHIPS, height, STA), jnp.bfloat16),
        in_specs=[SMEM if arg.dtype == jnp.int32 else VMEM for arg in args],
        out_specs=VMEM,
        compiler_params=pltpu.CompilerParams(vmem_limit_bytes=4 * MIB),
        name="rows",
    )(*args)


def choose_kernel(partners_ref, *refs):
    blocks, out_ref = refs[:-1], refs[-1]
    for q in range(SLOTS):
        rows = slice(q * SENT, (q + 1) * SENT)
        block, target, _ = partner(partners_ref, q)
        by = jnp.where(target < 0, 0, target - block)

        @pl.when(by == 0)
        def _():
            out_ref[rows] = jnp.zeros((SENT, STA), jnp.bfloat16)

        for step, ref in zip((-1, 1, -2, 2), blocks):

            @pl.when(by == step)
            def _():
                out_ref[rows] = ref[...]


def chosen(partners, blocks):
    return pl.pallas_call(
        choose_kernel,
        out_shape=jax.ShapeDtypeStruct((SLOTS * SENT, STA), jnp.bfloat16),
        in_specs=[SMEM] + [VMEM] * len(blocks),
        out_specs=VMEM,
        compiler_params=pltpu.CompilerParams(vmem_limit_bytes=4 * MIB),
        name="choose",
    )(partners, *blocks)


def lag_tables():
    lag = lax.broadcasted_iota(jnp.int32, (LPAD, COLS), 0) - LAG
    column = lax.broadcasted_iota(jnp.int32, (LPAD, COLS), 1)
    harmonic = jnp.where(column < BINS, column, column - BINS) + 1
    turns = (lag * harmonic).astype(jnp.float32) * (1.0 / WIN)
    phase = (turns - jnp.round(turns)) * (2.0 * math.pi)
    kept = lag <= LAG
    sine = jnp.where(column < BINS, -jnp.sin(phase), jnp.sin(phase))
    return jnp.where(kept, jnp.cos(phase), 0.0), jnp.where(kept, sine, 0.0)


def turn_kernel(own_ref, out_ref, mask_ref, held):
    _, chip, core = place()
    cosine, sine = (jnp.concatenate([table, table], axis=0).astype(jnp.bfloat16) for table in lag_tables())
    upper = lax.broadcasted_iota(jnp.int32, (16, COLS), 0) < 8

    def two(rows, k):
        first, second = (jnp.broadcast_to(rows[m : m + 1], (16, COLS)) for m in (k, k + 1))
        both = jnp.where(upper, first, second).astype(jnp.bfloat16)
        first, second = first.astype(jnp.bfloat16), second.astype(jnp.bfloat16)
        return jnp.concatenate([first] * (LPAD // 16) + [both] + [second] * (LPAD // 16), axis=0)

    for half in range(2):
        for d, by in enumerate(TURNS):
            source = lax.rem(chip + CHIPS - by, CHIPS)
            for h, whose in enumerate((1 - core, core)):
                here = slice(h * ROW_BLOCK, (h + 1) * ROW_BLOCK)
                for part in range(2):
                    start = pl.multiple_of((half * 2 + part) * CHIP_ROWS + whose * ROW_BLOCK, ROW_BLOCK)
                    rows = own_ref[source, pl.ds(start, ROW_BLOCK)]
                    held[d, here, part * STA : (part + 1) * STA] = rows.astype(jnp.float32)
        mask = held[0, :, WHITE:]
        for d in range(1, CHIPS):
            mask += pltpu.roll(held[d, :, WHITE:], d * MASK_ROWS, 1)
        mask_ref[half] = mask.astype(jnp.bfloat16)

        def eight(i, carry):
            stations = pl.ds(pl.multiple_of(i * 8, 8), 8)
            for d in range(CHIPS):
                for g in range(WHITE // COLS):
                    block = held[d, stations, g * COLS : (g + 1) * COLS]
                    swapped = pltpu.roll(block, BINS, 1)
                    lanes = slice(d * WHITE + g * COLS, d * WHITE + (g + 1) * COLS)
                    for k in range(0, 8, 2):
                        at = pl.multiple_of(i * 8 * LPAD + k * LPAD, 2 * LPAD)
                        out_ref[half, pl.ds(at, 2 * LPAD), lanes] = two(block, k) * cosine + two(swapped, k) * sine
            return carry

        lax.fori_loop(0, CHIP_ROWS // 8, eight, 0)


def turned_rows(own):
    height = CHIP_ROWS * LPAD
    return pl.pallas_call(
        turn_kernel,
        out_shape=[
            jax.ShapeDtypeStruct((2, height, DEEP), jnp.bfloat16),
            jax.ShapeDtypeStruct((2, CHIP_ROWS, 128), jnp.bfloat16),
        ],
        in_specs=[VMEM],
        out_specs=[VMEM, VMEM],
        scratch_shapes=[pltpu.VMEM((CHIPS, CHIP_ROWS, WIDE), jnp.float32)],
        compiler_params=pltpu.CompilerParams(vmem_limit_bytes=18 * MIB),
        cost_estimate=pl.CostEstimate(flops=6 * height * DEEP, bytes_accessed=4 * height * DEEP, transcendentals=0),
        name="turn",
    )(own)


def lags_kernel(groups, first, count, has_acc, partners_ref, turned_ref, valid_ref, *refs):
    acc_ref = refs[-2] if has_acc else None
    out_ref = refs[-1]
    taken, at = [], 0
    for half, low, high in groups:
        taken.append((half, low, high, refs[at : at + high - low]))
        at += high - low

    def half_of(q, half):
        return (partner(partners_ref, q)[2] + half) % 2

    def tile(i, carry):
        source = pl.ds(pl.multiple_of(first * LPAD + i * TILE, TILE), TILE)
        target = pl.ds(pl.multiple_of(i * TILE, TILE), TILE)
        for q in range(SLOTS):
            lanes = slice(q * STA, (q + 1) * STA)
            total = acc_ref[source, lanes] if has_acc else 0.0
            for half, low, high, far in taken:
                rows = jnp.concatenate([ref[q * SENT : q * SENT + WHITE] for ref in far], axis=0)
                turned = turned_ref[half_of(q, half), source, low * WHITE : high * WHITE]
                total += jnp.dot(turned, rows, preferred_element_type=jnp.float32)
            out_ref[target, lanes] = total.astype(out_ref.dtype)
        return carry

    lax.fori_loop(0, count * LPAD // TILE, tile, 0)
    for q in range(SLOTS):
        lanes = slice(q * STA, (q + 1) * STA)
        tally = 0.0
        for half, low, high, far in taken:
            mask = jnp.concatenate([ref[q * SENT + WHITE : (q + 1) * SENT] for ref in far], axis=0)
            valid = valid_ref[half_of(q, half), first : first + count]
            valid = valid[:, low * MASK_ROWS : high * MASK_ROWS]
            tally += jnp.dot(valid, mask, preferred_element_type=jnp.float32)
        for m in range(count):
            row = m * LPAD + TALLY_ROW
            value = tally[m : m + 1]
            if has_acc:
                value += acc_ref[first * LPAD + row : first * LPAD + row + 1, lanes]
            out_ref[row : row + 1, lanes] = value.astype(out_ref.dtype)


def into_lags(partners, own, groups, first, count, acc=None, dtype=jnp.float32):
    far = [piece for _, _, pieces in groups for piece in pieces]
    args = [partners, *own, *far] + ([] if acc is None else [acc])
    spans = tuple((half, low, low + len(pieces)) for half, low, pieces in groups)
    return pl.pallas_call(
        functools.partial(lags_kernel, spans, first, count, acc is not None),
        out_shape=jax.ShapeDtypeStruct((count * LPAD, SLOTS * STA), dtype),
        in_specs=[SMEM] + [VMEM] * (len(args) - 1),
        out_specs=VMEM,
        compiler_params=pltpu.CompilerParams(vmem_limit_bytes=8 * MIB),
        cost_estimate=pl.CostEstimate(
            flops=2 * count * LPAD * SLOTS * STA * WHITE * len(far),
            bytes_accessed=4 * count * LPAD * SLOTS * STA,
            transcendentals=0,
        ),
        name="lags",
    )(*args)


def combine_kernel(mine_ref, theirs_ref, out_hbm, out, sems):
    parts = sems.shape[0]
    step = out.shape[0] // parts
    copies = []
    for i in range(parts):
        for m in range(i * step, (i + 1) * step):
            rows = slice(m * LPAD, (m + 1) * LPAD)
            total = mine_ref[rows] + theirs_ref[rows].astype(jnp.float32)
            result = total[:LAGS] / jnp.maximum(total[TALLY_ROW : TALLY_ROW + 1], 1.0)
            for q in range(SLOTS):
                out[m, :, q] = result[:, q * STA : (q + 1) * STA]
        here = pl.ds(i * step, step)
        copies.append(pltpu.make_async_copy(out.at[here], out_hbm.at[here], sems.at[i]))
        copies[-1].start()
    for copy in copies:
        copy.wait()


def combined(mine, theirs):
    shape = (mine.shape[0] // LPAD, LAGS, SLOTS, STA)
    out = pl.pallas_call(
        combine_kernel,
        out_shape=jax.ShapeDtypeStruct(shape, jnp.float32),
        in_specs=[VMEM, VMEM],
        out_specs=ANY,
        scratch_shapes=[pltpu.VMEM(shape, jnp.float32), pltpu.SemaphoreType.DMA((8,))],
        compiler_params=pltpu.CompilerParams(vmem_limit_bytes=8 * MIB),
        name="combine",
    )(mine, theirs)
    return out.transpose(0, 2, 1, 3)


def body(records, validity, partners):
    partners = partners.T

    def neighbours(white):
        back, on = send(white, to_block(1)), send(white, to_block(-1))
        return [back, on, send(back, to_block(1)), send(on, to_block(-1))]

    def spread(held):
        return [held] + [send(held, to_chip(by)) for by in TURNS[1:]]

    white = whitened(records, validity)
    other = send(white, to_other_half)
    rows = by_rows(first_rows_kernel, OWN // 2, partners, white)
    rows, other = lax.optimization_barrier((rows, other))
    far, other_far = spread(chosen(partners, neighbours(white))), spread(chosen(partners, neighbours(other)))
    own = by_rows(own_kernel, OWN, rows, other)
    own = turned_rows(lax.all_to_all(own, "tm", 0, 0, axis_index_groups=CHIP_GROUPS, tiled=True))

    acc = into_lags(partners, own, [(0, 0, far)], 0, CHIP_ROWS)
    last = functools.partial(into_lags, partners, own, [(1, 0, other_far)], acc=acc)
    theirs = send(last(0, ROW_BLOCK, dtype=jnp.bfloat16), to_core)
    return combined(last(ROW_BLOCK, ROW_BLOCK), theirs)


def solution(mesh):
    return jax.shard_map(
        body,
        mesh=mesh,
        in_specs=(P("sta", "tm"), P("sta", "tm"), P()),
        out_specs=P(("sta", "tm"), None, None, None),
        check_vma=False,
    )
```

```python
import functools
import math

import jax
import jax.numpy as jnp
import numpy as np
from jax import lax
from jax.experimental import pallas as pl
from jax.experimental.pallas import tpu as pltpu
from jax.sharding import PartitionSpec as P

WIN = 600
BINS = 64
LAG = 32
SLOTS = 2
STA = 256
BLOCKS = 32
TM = 16
HALF = 8
CHIPS = 4
COLS = 2 * BINS
LAGS = 2 * LAG + 1
LPAD = 72
TALLY_ROW = LAGS
MASK_ROWS = 16
ROW_BLOCK = 128 // HALF
CHIP_ROWS = 2 * ROW_BLOCK
WHITE = 3 * COLS
SENT = WHITE + MASK_ROWS
WIDE = WHITE + 128
OWN = 4 * CHIP_ROWS
TURNS = (0, 1, -1, 2)
TILE = 16 * LPAD
DEEP = CHIPS * WHITE
SPAN = 616
AXES = ("sta", "tm")
MIB = 1 << 20


def forward_table():
    sample = np.arange(WIN)
    harmonic = np.arange(1, BINS + 1)
    residue = sample[:, None] * harmonic[None, :] % WIN
    phase = residue.astype(np.float32) * np.float32(2.0 * math.pi / WIN)
    taper = np.float32(0.5) - np.float32(0.5) * np.cos(
        (sample.astype(np.float32) + np.float32(0.5)) * np.float32(2.0 * math.pi / WIN)
    )
    table = np.concatenate([taper[:, None] * np.cos(phase), -taper[:, None] * np.sin(phase)], axis=1)
    return (table * np.float32(1.0 / math.sqrt(WIN))).astype(jnp.bfloat16)


def window_start(w):
    return w * (WIN // 16 * 16)


def window_tables(win_dev):
    table = forward_table()
    out = np.zeros((win_dev, COLS, SPAN), table.dtype)
    for w in range(win_dev):
        at = w * WIN - window_start(w)
        out[w, :, at : at + WIN] = table.T
    return out


def band_average():
    bins = np.arange(BINS)
    nearby = (np.abs(bins[:, None] - bins[None, :]) <= 2).astype(np.float32)
    return np.ascontiguousarray((nearby / nearby.sum(axis=0, keepdims=True)).T)


def routes(target):
    pairs = []
    for b in range(BLOCKS):
        for t in range(TM):
            there = target(b, t)
            if there is not None:
                pairs.append((b * TM + t, there[0] * TM + there[1]))
    return pairs


def to_other_half(b, t):
    return b, (t + HALF) % TM


def to_block(by):
    def target(b, t):
        nb = b + by
        if not 0 <= nb < BLOCKS:
            return None
        return nb, t if nb // 8 == b // 8 else (t + HALF) % TM

    return target


def to_chip(by):
    return lambda b, t: (b, t // HALF * HALF + (t % HALF // 2 + by) % CHIPS * 2 + t % 2)


def to_core(b, t):
    return b, t ^ 1


def send(array, target):
    return lax.ppermute(array, AXES, routes(target))


CHIP_GROUPS = [[z * HALF + 2 * i + c for i in range(CHIPS)] for z in range(TM // HALF) for c in range(2)]


VMEM = pl.BlockSpec(memory_space=pltpu.VMEM)
SMEM = pl.BlockSpec(memory_space=pltpu.SMEM)
ANY = pl.BlockSpec(memory_space=pl.ANY)


def place():
    index = lax.axis_index("tm")
    return index // HALF, index % HALF // 2, index % 2


def partner(partners_ref, q):
    block = lax.axis_index("sta")
    target = partners_ref[q, block]
    return block, target, jnp.where(target // 8 == block // 8, 0, 1)


def whiten_kernel(rec_hbm, mask_hbm, avg_hbm, table_hbm, out_ref, rec, mask_in, avg, table, sems):
    win_dev = table_hbm.shape[0]
    copies = [pltpu.make_async_copy(mask_hbm, mask_in, sems.at[0]), pltpu.make_async_copy(avg_hbm, avg, sems.at[1])]
    for w in range(win_dev):
        copies.append(pltpu.make_async_copy(table_hbm.at[w], table.at[w], sems.at[2 + 2 * w]))
        samples = pl.ds(window_start(w), SPAN)
        copies.append(pltpu.make_async_copy(rec_hbm.at[samples], rec.at[w], sems.at[3 + 2 * w]))
    for copy in copies:
        copy.start()
    copies[0].wait()
    copies[1].wait()
    mask = mask_in[...].astype(jnp.float32)
    for w in range(win_dev):
        copies[2 + 2 * w].wait()
        copies[3 + 2 * w].wait()
        spectra = jnp.dot(table[w], rec[w], preferred_element_type=jnp.float32)
        real, imag = spectra[:BINS], spectra[BINS:]
        power = real * real + imag * imag
        smooth = jnp.dot(avg[...], power, precision=lax.Precision.HIGHEST, preferred_element_type=jnp.float32)
        scale = mask[w : w + 1] / jnp.sqrt(smooth + 0.05)
        out_ref[w * COLS : w * COLS + BINS] = (real * scale).astype(jnp.bfloat16)
        out_ref[w * COLS + BINS : (w + 1) * COLS] = (imag * scale).astype(jnp.bfloat16)
    empty = jnp.zeros((MASK_ROWS - win_dev, STA), jnp.float32)
    out_ref[WHITE:] = jnp.concatenate([mask, empty], axis=0).astype(jnp.bfloat16)


def whitened(records, validity):
    rows, win_dev = validity.shape
    return pl.pallas_call(
        whiten_kernel,
        out_shape=jax.ShapeDtypeStruct((SENT, rows), jnp.bfloat16),
        in_specs=[ANY] * 4,
        out_specs=VMEM,
        scratch_shapes=[
            pltpu.VMEM((win_dev, SPAN, rows), records.dtype),
            pltpu.VMEM((win_dev, rows), jnp.int32),
            pltpu.VMEM((BINS, BINS), jnp.float32),
            pltpu.VMEM((win_dev, COLS, SPAN), jnp.bfloat16),
            pltpu.SemaphoreType.DMA((2 + 2 * win_dev,)),
        ],
        compiler_params=pltpu.CompilerParams(vmem_limit_bytes=60 * MIB),
        name="whiten",
    )(records.T, validity.T, band_average(), window_tables(win_dev))


def first_rows_kernel(partners_ref, white_ref, out_ref):
    del partners_ref
    rows_kernel(white_ref, out_ref)


def rows_kernel(white_ref, out_ref, half=0):
    lanes = pl.ds(pl.multiple_of(place()[0] * 128, 128), 128)
    blocks = [white_ref[g * COLS : (g + 1) * COLS, lanes].astype(jnp.float32) for g in range(WHITE // COLS)]
    mask = white_ref[WHITE:SENT, lanes].astype(jnp.float32)
    blocks.append(jnp.concatenate([mask, jnp.zeros((128 - MASK_ROWS, 128), jnp.float32)], axis=0))
    for g, block in enumerate(blocks):
        rows = block.T.astype(jnp.bfloat16)
        at = (half * 2 + g // 2) * CHIP_ROWS
        for x in range(CHIPS):
            piece = rows[x * CHIP_ROWS : (x + 1) * CHIP_ROWS]
            out_ref[x, at : at + CHIP_ROWS, g % 2 * 128 : (g % 2 + 1) * 128] = piece


def own_kernel(first_ref, other_ref, out_ref):
    out_ref[:, : OWN // 2] = first_ref[...]
    rows_kernel(other_ref, out_ref, 1)


def by_rows(kernel, height, *args):
    return pl.pallas_call(
        kernel,
        out_shape=jax.ShapeDtypeStruct((CHIPS, height, STA), jnp.bfloat16),
        in_specs=[SMEM if arg.dtype == jnp.int32 else VMEM for arg in args],
        out_specs=VMEM,
        compiler_params=pltpu.CompilerParams(vmem_limit_bytes=4 * MIB),
        name="rows",
    )(*args)


def choose_kernel(partners_ref, *refs):
    blocks, out_ref = refs[:-1], refs[-1]
    for q in range(SLOTS):
        rows = slice(q * SENT, (q + 1) * SENT)
        block, target, _ = partner(partners_ref, q)
        by = jnp.where(target < 0, 0, target - block)

        @pl.when(by == 0)
        def _():
            out_ref[rows] = jnp.zeros((SENT, STA), jnp.bfloat16)

        for step, ref in zip((-1, 1, -2, 2), blocks):

            @pl.when(by == step)
            def _():
                out_ref[rows] = ref[...]


def chosen(partners, blocks):
    return pl.pallas_call(
        choose_kernel,
        out_shape=jax.ShapeDtypeStruct((SLOTS * SENT, STA), jnp.bfloat16),
        in_specs=[SMEM] + [VMEM] * len(blocks),
        out_specs=VMEM,
        compiler_params=pltpu.CompilerParams(vmem_limit_bytes=4 * MIB),
        name="choose",
    )(partners, *blocks)


def lag_tables():
    lag = lax.broadcasted_iota(jnp.int32, (LPAD, COLS), 0) - LAG
    column = lax.broadcasted_iota(jnp.int32, (LPAD, COLS), 1)
    harmonic = jnp.where(column < BINS, column, column - BINS) + 1
    turns = (lag * harmonic).astype(jnp.float32) * (1.0 / WIN)
    phase = (turns - jnp.round(turns)) * (2.0 * math.pi)
    kept = lag <= LAG
    sine = jnp.where(column < BINS, -jnp.sin(phase), jnp.sin(phase))
    return jnp.where(kept, jnp.cos(phase), 0.0), jnp.where(kept, sine, 0.0)


def turn_kernel(own_ref, out_ref, mask_ref, held):
    _, chip, core = place()
    cosine, sine = lag_tables()
    for half in range(2):
        for d, by in enumerate(TURNS):
            source = lax.rem(chip + CHIPS - by, CHIPS)
            for h, whose in enumerate((1 - core, core)):
                here = slice(h * ROW_BLOCK, (h + 1) * ROW_BLOCK)
                for part in range(2):
                    start = pl.multiple_of((half * 2 + part) * CHIP_ROWS + whose * ROW_BLOCK, ROW_BLOCK)
                    rows = own_ref[source, pl.ds(start, ROW_BLOCK)]
                    held[d, here, part * STA : (part + 1) * STA] = rows.astype(jnp.float32)
        mask = held[0, :, WHITE:]
        for d in range(1, CHIPS):
            mask += pltpu.roll(held[d, :, WHITE:], d * MASK_ROWS, 1)
        mask_ref[half] = mask.astype(jnp.bfloat16)

        def eight(i, carry):
            stations = pl.ds(pl.multiple_of(i * 8, 8), 8)
            for d in range(CHIPS):
                for g in range(WHITE // COLS):
                    block = held[d, stations, g * COLS : (g + 1) * COLS]
                    swapped = pltpu.roll(block, BINS, 1)
                    lanes = slice(d * WHITE + g * COLS, d * WHITE + (g + 1) * COLS)
                    for k in range(0, 8, 2):
                        turned = [block[m : m + 1] * cosine + swapped[m : m + 1] * sine for m in (k, k + 1)]
                        at = pl.multiple_of(i * 8 * LPAD + k * LPAD, 2 * LPAD)
                        out_ref[half, pl.ds(at, 2 * LPAD), lanes] = jnp.concatenate(turned, axis=0).astype(jnp.bfloat16)
            return carry

        lax.fori_loop(0, CHIP_ROWS // 8, eight, 0)


def turned_rows(own):
    height = CHIP_ROWS * LPAD
    return pl.pallas_call(
        turn_kernel,
        out_shape=[
            jax.ShapeDtypeStruct((2, height, DEEP), jnp.bfloat16),
            jax.ShapeDtypeStruct((2, CHIP_ROWS, 128), jnp.bfloat16),
        ],
        in_specs=[VMEM],
        out_specs=[VMEM, VMEM],
        scratch_shapes=[pltpu.VMEM((CHIPS, CHIP_ROWS, WIDE), jnp.float32)],
        compiler_params=pltpu.CompilerParams(vmem_limit_bytes=18 * MIB),
        cost_estimate=pl.CostEstimate(flops=6 * height * DEEP, bytes_accessed=4 * height * DEEP, transcendentals=0),
        name="turn",
    )(own)


def lags_kernel(groups, first, count, has_acc, partners_ref, turned_ref, valid_ref, *refs):
    acc_ref = refs[-2] if has_acc else None
    out_ref = refs[-1]
    taken, at = [], 0
    for half, low, high in groups:
        taken.append((half, low, high, refs[at : at + high - low]))
        at += high - low

    def half_of(q, half):
        return (partner(partners_ref, q)[2] + half) % 2

    def tile(i, carry):
        source = pl.ds(pl.multiple_of(first * LPAD + i * TILE, TILE), TILE)
        target = pl.ds(pl.multiple_of(i * TILE, TILE), TILE)
        for q in range(SLOTS):
            lanes = slice(q * STA, (q + 1) * STA)
            total = acc_ref[source, lanes] if has_acc else 0.0
            for half, low, high, far in taken:
                rows = jnp.concatenate([ref[q * SENT : q * SENT + WHITE] for ref in far], axis=0)
                turned = turned_ref[half_of(q, half), source, low * WHITE : high * WHITE]
                total += jnp.dot(turned, rows, preferred_element_type=jnp.float32)
            out_ref[target, lanes] = total.astype(out_ref.dtype)
        return carry

    lax.fori_loop(0, count * LPAD // TILE, tile, 0)
    for q in range(SLOTS):
        lanes = slice(q * STA, (q + 1) * STA)
        tally = 0.0
        for half, low, high, far in taken:
            mask = jnp.concatenate([ref[q * SENT + WHITE : (q + 1) * SENT] for ref in far], axis=0)
            valid = valid_ref[half_of(q, half), first : first + count]
            valid = valid[:, low * MASK_ROWS : high * MASK_ROWS]
            tally += jnp.dot(valid, mask, preferred_element_type=jnp.float32)
        for m in range(count):
            row = m * LPAD + TALLY_ROW
            value = tally[m : m + 1]
            if has_acc:
                value += acc_ref[first * LPAD + row : first * LPAD + row + 1, lanes]
            out_ref[row : row + 1, lanes] = value.astype(out_ref.dtype)


def into_lags(partners, own, groups, first, count, acc=None, dtype=jnp.float32):
    far = [piece for _, _, pieces in groups for piece in pieces]
    args = [partners, *own, *far] + ([] if acc is None else [acc])
    spans = tuple((half, low, low + len(pieces)) for half, low, pieces in groups)
    return pl.pallas_call(
        functools.partial(lags_kernel, spans, first, count, acc is not None),
        out_shape=jax.ShapeDtypeStruct((count * LPAD, SLOTS * STA), dtype),
        in_specs=[SMEM] + [VMEM] * (len(args) - 1),
        out_specs=VMEM,
        compiler_params=pltpu.CompilerParams(vmem_limit_bytes=8 * MIB),
        cost_estimate=pl.CostEstimate(
            flops=2 * count * LPAD * SLOTS * STA * WHITE * len(far),
            bytes_accessed=4 * count * LPAD * SLOTS * STA,
            transcendentals=0,
        ),
        name="lags",
    )(*args)


def combine_kernel(mine_ref, theirs_ref, out_hbm, out, sems):
    parts = sems.shape[0]
    step = out.shape[0] // parts
    copies = []
    for i in range(parts):
        for m in range(i * step, (i + 1) * step):
            rows = slice(m * LPAD, (m + 1) * LPAD)
            total = mine_ref[rows] + theirs_ref[rows].astype(jnp.float32)
            result = total[:LAGS] / jnp.maximum(total[TALLY_ROW : TALLY_ROW + 1], 1.0)
            for q in range(SLOTS):
                out[m, :, q] = result[:, q * STA : (q + 1) * STA]
        here = pl.ds(i * step, step)
        copies.append(pltpu.make_async_copy(out.at[here], out_hbm.at[here], sems.at[i]))
        copies[-1].start()
    for copy in copies:
        copy.wait()


def combined(mine, theirs):
    shape = (mine.shape[0] // LPAD, LAGS, SLOTS, STA)
    out = pl.pallas_call(
        combine_kernel,
        out_shape=jax.ShapeDtypeStruct(shape, jnp.float32),
        in_specs=[VMEM, VMEM],
        out_specs=ANY,
        scratch_shapes=[pltpu.VMEM(shape, jnp.float32), pltpu.SemaphoreType.DMA((8,))],
        compiler_params=pltpu.CompilerParams(vmem_limit_bytes=8 * MIB),
        name="combine",
    )(mine, theirs)
    return out.transpose(0, 2, 1, 3)


def body(records, validity, partners):
    partners = partners.T

    def neighbours(white):
        back, on = send(white, to_block(1)), send(white, to_block(-1))
        return [back, on, send(back, to_block(1)), send(on, to_block(-1))]

    def spread(held):
        return [held] + [send(held, to_chip(by)) for by in TURNS[1:]]

    white = whitened(records, validity)
    other = send(white, to_other_half)
    rows = by_rows(first_rows_kernel, OWN // 2, partners, white)
    rows, other = lax.optimization_barrier((rows, other))
    far, other_far = spread(chosen(partners, neighbours(white))), spread(chosen(partners, neighbours(other)))
    own = by_rows(own_kernel, OWN, rows, other)
    own = turned_rows(lax.all_to_all(own, "tm", 0, 0, axis_index_groups=CHIP_GROUPS, tiled=True))

    acc = into_lags(partners, own, [(0, 0, far)], 0, CHIP_ROWS)
    last = functools.partial(into_lags, partners, own, [(1, 0, other_far)], acc=acc)
    theirs = send(last(0, ROW_BLOCK, dtype=jnp.bfloat16), to_core)
    return combined(last(ROW_BLOCK, ROW_BLOCK), theirs)


def solution(mesh):
    return jax.shard_map(
        body,
        mesh=mesh,
        in_specs=(P("sta", "tm"), P("sta", "tm"), P()),
        out_specs=P(("sta", "tm"), None, None, None),
        check_vma=False,
    )
```

```python
import functools
import math

import jax
import jax.numpy as jnp
import numpy as np
from jax import lax
from jax.experimental import pallas as pl
from jax.experimental.pallas import tpu as pltpu
from jax.sharding import PartitionSpec as P

WIN = 600
BINS = 64
LAG = 32
SLOTS = 2
STA = 256
BLOCKS = 32
TM = 16
HALF = 8
CHIPS = 4
COLS = 2 * BINS
LAGS = 2 * LAG + 1
LPAD = 72
TALLY_ROW = LAGS
MASK_ROWS = 16
ROW_BLOCK = 128 // HALF
CHIP_ROWS = 2 * ROW_BLOCK
WHITE = 3 * COLS
SENT = WHITE + MASK_ROWS
WIDE = WHITE + 128
OWN = 4 * CHIP_ROWS
TURNS = (0, 1, -1, 2)
TILE = 16 * LPAD
DEEP = CHIPS * WHITE
SPAN = 616
AXES = ("sta", "tm")
MIB = 1 << 20


def forward_table():
    sample = np.arange(WIN)
    harmonic = np.arange(1, BINS + 1)
    residue = sample[:, None] * harmonic[None, :] % WIN
    phase = residue.astype(np.float32) * np.float32(2.0 * math.pi / WIN)
    taper = np.float32(0.5) - np.float32(0.5) * np.cos(
        (sample.astype(np.float32) + np.float32(0.5)) * np.float32(2.0 * math.pi / WIN)
    )
    table = np.concatenate([taper[:, None] * np.cos(phase), -taper[:, None] * np.sin(phase)], axis=1)
    return (table * np.float32(1.0 / math.sqrt(WIN))).astype(jnp.bfloat16)


def window_start(w):
    return w * (WIN // 16 * 16)


def window_tables(win_dev):
    table = forward_table()
    out = np.zeros((win_dev, COLS, SPAN), table.dtype)
    for w in range(win_dev):
        at = w * WIN - window_start(w)
        out[w, :, at : at + WIN] = table.T
    return out


def band_average():
    bins = np.arange(BINS)
    nearby = (np.abs(bins[:, None] - bins[None, :]) <= 2).astype(np.float32)
    return np.ascontiguousarray((nearby / nearby.sum(axis=0, keepdims=True)).T)


def routes(target):
    pairs = []
    for b in range(BLOCKS):
        for t in range(TM):
            there = target(b, t)
            if there is not None:
                pairs.append((b * TM + t, there[0] * TM + there[1]))
    return pairs


def to_other_half(b, t):
    return b, (t + HALF) % TM


def to_block(by):
    def target(b, t):
        nb = b + by
        if not 0 <= nb < BLOCKS:
            return None
        return nb, t if nb // 8 == b // 8 else (t + HALF) % TM

    return target


def to_chip(by):
    return lambda b, t: (b, t // HALF * HALF + (t % HALF // 2 + by) % CHIPS * 2 + t % 2)


def to_core(b, t):
    return b, t ^ 1


def send(array, target):
    return lax.ppermute(array, AXES, routes(target))


CHIP_GROUPS = [[z * HALF + 2 * i + c for i in range(CHIPS)] for z in range(TM // HALF) for c in range(2)]


VMEM = pl.BlockSpec(memory_space=pltpu.VMEM)
SMEM = pl.BlockSpec(memory_space=pltpu.SMEM)
ANY = pl.BlockSpec(memory_space=pl.ANY)


def place():
    index = lax.axis_index("tm")
    return index // HALF, index % HALF // 2, index % 2


def partner(partners_ref, q):
    block = lax.axis_index("sta")
    target = partners_ref[q, block]
    return block, target, jnp.where(target // 8 == block // 8, 0, 1)


def whiten_kernel(rec_hbm, mask_hbm, avg_hbm, table_hbm, out_hbm, out_ref, rec, mask_in, avg, table, sems, out_sems):
    win_dev = table_hbm.shape[0]
    copies = [pltpu.make_async_copy(mask_hbm, mask_in, sems.at[0]), pltpu.make_async_copy(avg_hbm, avg, sems.at[1])]
    for w in range(win_dev):
        copies.append(pltpu.make_async_copy(table_hbm.at[w], table.at[w], sems.at[2 + 2 * w]))
        samples = pl.ds(window_start(w), SPAN)
        copies.append(pltpu.make_async_copy(rec_hbm.at[samples], rec.at[w], sems.at[3 + 2 * w]))
    for copy in copies:
        copy.start()
    copies[0].wait()
    copies[1].wait()
    mask = mask_in[...].astype(jnp.float32)
    empty = jnp.zeros((MASK_ROWS - win_dev, STA), jnp.float32)
    out_ref[WHITE:] = jnp.concatenate([mask, empty], axis=0).astype(jnp.bfloat16)
    leaving = []

    def leave(rows):
        leaving.append(pltpu.make_async_copy(out_ref.at[rows], out_hbm.at[rows], out_sems.at[len(leaving)]))
        leaving[-1].start()

    leave(pl.ds(WHITE, MASK_ROWS))
    for w in range(win_dev):
        copies[2 + 2 * w].wait()
        copies[3 + 2 * w].wait()
        spectra = jnp.dot(table[w], rec[w], preferred_element_type=jnp.float32)
        real, imag = spectra[:BINS], spectra[BINS:]
        power = real * real + imag * imag
        smooth = jnp.dot(avg[...], power, precision=lax.Precision.HIGHEST, preferred_element_type=jnp.float32)
        scale = mask[w : w + 1] / jnp.sqrt(smooth + 0.05)
        out_ref[w * COLS : w * COLS + BINS] = (real * scale).astype(jnp.bfloat16)
        out_ref[w * COLS + BINS : (w + 1) * COLS] = (imag * scale).astype(jnp.bfloat16)
        leave(pl.ds(w * COLS, COLS))
    for copy in leaving:
        copy.wait()


def whitened(records, validity):
    rows, win_dev = validity.shape
    return pl.pallas_call(
        whiten_kernel,
        out_shape=jax.ShapeDtypeStruct((SENT, rows), jnp.bfloat16),
        in_specs=[ANY] * 4,
        out_specs=ANY,
        scratch_shapes=[
            pltpu.VMEM((SENT, rows), jnp.bfloat16),
            pltpu.VMEM((win_dev, SPAN, rows), records.dtype),
            pltpu.VMEM((win_dev, rows), jnp.int32),
            pltpu.VMEM((BINS, BINS), jnp.float32),
            pltpu.VMEM((win_dev, COLS, SPAN), jnp.bfloat16),
            pltpu.SemaphoreType.DMA((2 + 2 * win_dev,)),
            pltpu.SemaphoreType.DMA((1 + win_dev,)),
        ],
        compiler_params=pltpu.CompilerParams(vmem_limit_bytes=60 * MIB),
        name="whiten",
    )(records.T, validity.T, band_average(), window_tables(win_dev))


def first_rows_kernel(partners_ref, white_ref, out_ref):
    del partners_ref
    rows_kernel(white_ref, out_ref)


def rows_kernel(white_ref, out_ref, half=0):
    lanes = pl.ds(pl.multiple_of(place()[0] * 128, 128), 128)
    blocks = [white_ref[g * COLS : (g + 1) * COLS, lanes].astype(jnp.float32) for g in range(WHITE // COLS)]
    mask = white_ref[WHITE:SENT, lanes].astype(jnp.float32)
    blocks.append(jnp.concatenate([mask, jnp.zeros((128 - MASK_ROWS, 128), jnp.float32)], axis=0))
    for g, block in enumerate(blocks):
        rows = block.T.astype(jnp.bfloat16)
        at = (half * 2 + g // 2) * CHIP_ROWS
        for x in range(CHIPS):
            piece = rows[x * CHIP_ROWS : (x + 1) * CHIP_ROWS]
            out_ref[x, at : at + CHIP_ROWS, g % 2 * 128 : (g % 2 + 1) * 128] = piece


def own_kernel(first_ref, other_ref, out_ref):
    out_ref[:, : OWN // 2] = first_ref[...]
    rows_kernel(other_ref, out_ref, 1)


def by_rows(kernel, height, *args):
    return pl.pallas_call(
        kernel,
        out_shape=jax.ShapeDtypeStruct((CHIPS, height, STA), jnp.bfloat16),
        in_specs=[SMEM if arg.dtype == jnp.int32 else VMEM for arg in args],
        out_specs=VMEM,
        compiler_params=pltpu.CompilerParams(vmem_limit_bytes=4 * MIB),
        name="rows",
    )(*args)


def choose_kernel(partners_ref, *refs):
    blocks, out_ref = refs[:-1], refs[-1]
    for q in range(SLOTS):
        rows = slice(q * SENT, (q + 1) * SENT)
        block, target, _ = partner(partners_ref, q)
        by = jnp.where(target < 0, 0, target - block)

        @pl.when(by == 0)
        def _():
            out_ref[rows] = jnp.zeros((SENT, STA), jnp.bfloat16)

        for step, ref in zip((-1, 1, -2, 2), blocks):

            @pl.when(by == step)
            def _():
                out_ref[rows] = ref[...]


def chosen(partners, blocks):
    return pl.pallas_call(
        choose_kernel,
        out_shape=jax.ShapeDtypeStruct((SLOTS * SENT, STA), jnp.bfloat16),
        in_specs=[SMEM] + [VMEM] * len(blocks),
        out_specs=VMEM,
        compiler_params=pltpu.CompilerParams(vmem_limit_bytes=4 * MIB),
        name="choose",
    )(partners, *blocks)


def lag_tables():
    lag = lax.broadcasted_iota(jnp.int32, (LPAD, COLS), 0) - LAG
    column = lax.broadcasted_iota(jnp.int32, (LPAD, COLS), 1)
    harmonic = jnp.where(column < BINS, column, column - BINS) + 1
    turns = (lag * harmonic).astype(jnp.float32) * (1.0 / WIN)
    phase = (turns - jnp.round(turns)) * (2.0 * math.pi)
    kept = lag <= LAG
    sine = jnp.where(column < BINS, -jnp.sin(phase), jnp.sin(phase))
    return jnp.where(kept, jnp.cos(phase), 0.0), jnp.where(kept, sine, 0.0)


def turn_kernel(own_ref, out_ref, mask_ref, held):
    _, chip, core = place()
    cosine, sine = (jnp.concatenate([table, table], axis=0).astype(jnp.bfloat16) for table in lag_tables())
    upper = lax.broadcasted_iota(jnp.int32, (16, COLS), 0) < 8

    def two(rows, k):
        first, second = (jnp.broadcast_to(rows[m : m + 1], (16, COLS)) for m in (k, k + 1))
        both = jnp.where(upper, first, second).astype(jnp.bfloat16)
        first, second = first.astype(jnp.bfloat16), second.astype(jnp.bfloat16)
        return jnp.concatenate([first] * (LPAD // 16) + [both] + [second] * (LPAD // 16), axis=0)

    for half in range(2):
        for d, by in enumerate(TURNS):
            source = lax.rem(chip + CHIPS - by, CHIPS)
            for h, whose in enumerate((1 - core, core)):
                here = slice(h * ROW_BLOCK, (h + 1) * ROW_BLOCK)
                for part in range(2):
                    start = pl.multiple_of((half * 2 + part) * CHIP_ROWS + whose * ROW_BLOCK, ROW_BLOCK)
                    rows = own_ref[source, pl.ds(start, ROW_BLOCK)]
                    held[d, here, part * STA : (part + 1) * STA] = rows.astype(jnp.float32)
        mask = held[0, :, WHITE:]
        for d in range(1, CHIPS):
            mask += pltpu.roll(held[d, :, WHITE:], d * MASK_ROWS, 1)
        mask_ref[half] = mask.astype(jnp.bfloat16)

        def eight(i, carry):
            stations = pl.ds(pl.multiple_of(i * 8, 8), 8)
            for d in range(CHIPS):
                for g in range(WHITE // COLS):
                    block = held[d, stations, g * COLS : (g + 1) * COLS]
                    swapped = pltpu.roll(block, BINS, 1)
                    lanes = slice(d * WHITE + g * COLS, d * WHITE + (g + 1) * COLS)
                    for k in range(0, 8, 2):
                        at = pl.multiple_of(i * 8 * LPAD + k * LPAD, 2 * LPAD)
                        out_ref[half, pl.ds(at, 2 * LPAD), lanes] = two(block, k) * cosine + two(swapped, k) * sine
            return carry

        lax.fori_loop(0, CHIP_ROWS // 8, eight, 0)


def turned_rows(own):
    height = CHIP_ROWS * LPAD
    return pl.pallas_call(
        turn_kernel,
        out_shape=[
            jax.ShapeDtypeStruct((2, height, DEEP), jnp.bfloat16),
            jax.ShapeDtypeStruct((2, CHIP_ROWS, 128), jnp.bfloat16),
        ],
        in_specs=[VMEM],
        out_specs=[VMEM, VMEM],
        scratch_shapes=[pltpu.VMEM((CHIPS, CHIP_ROWS, WIDE), jnp.float32)],
        compiler_params=pltpu.CompilerParams(vmem_limit_bytes=18 * MIB),
        cost_estimate=pl.CostEstimate(flops=6 * height * DEEP, bytes_accessed=4 * height * DEEP, transcendentals=0),
        name="turn",
    )(own)


def lags_kernel(groups, first, count, has_acc, partners_ref, turned_ref, valid_ref, *refs):
    acc_ref = refs[-2] if has_acc else None
    out_ref = refs[-1]
    taken, at = [], 0
    for half, low, high in groups:
        taken.append((half, low, high, refs[at : at + high - low]))
        at += high - low

    def half_of(q, half):
        return (partner(partners_ref, q)[2] + half) % 2

    def tile(i, carry):
        source = pl.ds(pl.multiple_of(first * LPAD + i * TILE, TILE), TILE)
        target = pl.ds(pl.multiple_of(i * TILE, TILE), TILE)
        for q in range(SLOTS):
            lanes = slice(q * STA, (q + 1) * STA)
            total = acc_ref[source, lanes] if has_acc else 0.0
            for half, low, high, far in taken:
                rows = jnp.concatenate([ref[q * SENT : q * SENT + WHITE] for ref in far], axis=0)
                turned = turned_ref[half_of(q, half), source, low * WHITE : high * WHITE]
                total += jnp.dot(turned, rows, preferred_element_type=jnp.float32)
            out_ref[target, lanes] = total.astype(out_ref.dtype)
        return carry

    lax.fori_loop(0, count * LPAD // TILE, tile, 0)
    for q in range(SLOTS):
        lanes = slice(q * STA, (q + 1) * STA)
        tally = 0.0
        for half, low, high, far in taken:
            mask = jnp.concatenate([ref[q * SENT + WHITE : (q + 1) * SENT] for ref in far], axis=0)
            valid = valid_ref[half_of(q, half), first : first + count]
            valid = valid[:, low * MASK_ROWS : high * MASK_ROWS]
            tally += jnp.dot(valid, mask, preferred_element_type=jnp.float32)
        for m in range(count):
            row = m * LPAD + TALLY_ROW
            value = tally[m : m + 1]
            if has_acc:
                value += acc_ref[first * LPAD + row : first * LPAD + row + 1, lanes]
            out_ref[row : row + 1, lanes] = value.astype(out_ref.dtype)


def into_lags(partners, own, groups, first, count, acc=None, dtype=jnp.float32):
    far = [piece for _, _, pieces in groups for piece in pieces]
    args = [partners, *own, *far] + ([] if acc is None else [acc])
    spans = tuple((half, low, low + len(pieces)) for half, low, pieces in groups)
    return pl.pallas_call(
        functools.partial(lags_kernel, spans, first, count, acc is not None),
        out_shape=jax.ShapeDtypeStruct((count * LPAD, SLOTS * STA), dtype),
        in_specs=[SMEM] + [VMEM] * (len(args) - 1),
        out_specs=VMEM,
        compiler_params=pltpu.CompilerParams(vmem_limit_bytes=8 * MIB),
        cost_estimate=pl.CostEstimate(
            flops=2 * count * LPAD * SLOTS * STA * WHITE * len(far),
            bytes_accessed=4 * count * LPAD * SLOTS * STA,
            transcendentals=0,
        ),
        name="lags",
    )(*args)


def combine_kernel(mine_ref, theirs_ref, out_hbm, out, sems):
    parts = sems.shape[0]
    step = out.shape[0] // parts
    copies = []
    for i in range(parts):
        for m in range(i * step, (i + 1) * step):
            rows = slice(m * LPAD, (m + 1) * LPAD)
            total = mine_ref[rows] + theirs_ref[rows].astype(jnp.float32)
            result = total[:LAGS] / jnp.maximum(total[TALLY_ROW : TALLY_ROW + 1], 1.0)
            for q in range(SLOTS):
                out[m, :, q] = result[:, q * STA : (q + 1) * STA]
        here = pl.ds(i * step, step)
        copies.append(pltpu.make_async_copy(out.at[here], out_hbm.at[here], sems.at[i]))
        copies[-1].start()
    for copy in copies:
        copy.wait()


def combined(mine, theirs):
    shape = (mine.shape[0] // LPAD, LAGS, SLOTS, STA)
    out = pl.pallas_call(
        combine_kernel,
        out_shape=jax.ShapeDtypeStruct(shape, jnp.float32),
        in_specs=[VMEM, VMEM],
        out_specs=ANY,
        scratch_shapes=[pltpu.VMEM(shape, jnp.float32), pltpu.SemaphoreType.DMA((8,))],
        compiler_params=pltpu.CompilerParams(vmem_limit_bytes=8 * MIB),
        name="combine",
    )(mine, theirs)
    return out.transpose(0, 2, 1, 3)


def body(records, validity, partners):
    partners = partners.T

    def neighbours(white):
        back, on = send(white, to_block(1)), send(white, to_block(-1))
        return [back, on, send(back, to_block(1)), send(on, to_block(-1))]

    def spread(held):
        return [held] + [send(held, to_chip(by)) for by in TURNS[1:]]

    white = whitened(records, validity)
    other = send(white, to_other_half)
    rows = by_rows(first_rows_kernel, OWN // 2, partners, white)
    rows, other = lax.optimization_barrier((rows, other))
    far, other_far = spread(chosen(partners, neighbours(white))), spread(chosen(partners, neighbours(other)))
    own = by_rows(own_kernel, OWN, rows, other)
    own = turned_rows(lax.all_to_all(own, "tm", 0, 0, axis_index_groups=CHIP_GROUPS, tiled=True))

    acc = into_lags(partners, own, [(0, 0, far)], 0, CHIP_ROWS)
    last = functools.partial(into_lags, partners, own, [(1, 0, other_far)], acc=acc)
    theirs = send(last(0, ROW_BLOCK, dtype=jnp.bfloat16), to_core)
    return combined(last(ROW_BLOCK, ROW_BLOCK), theirs)


def solution(mesh):
    return jax.shard_map(
        body,
        mesh=mesh,
        in_specs=(P("sta", "tm"), P("sta", "tm"), P()),
        out_specs=P(("sta", "tm"), None, None, None),
        check_vma=False,
    )
```
